32 devices in a mesh: groups: 2 (over y), atoms: 8 (over z, x), samples: 2 (over core).
Axes of the slice: x: 2, y: 2, z: 4, core: 2. Of those that a mesh axis runs over, the one named last changes fastest.
Arguments:
- act: bfloat16 [16, 10240, 128], P('samples', ('groups', 'atoms')), parts along dimension 1, may hold values from -6 to 6
- grad_out: bfloat16 [16, 10240, 128], P('samples', ('groups', 'atoms')), parts along dimension 1, may hold values from -6 to 6
- pair: bfloat16 [320, 32, 16, 128], P(('groups', 'atoms')), parts along dimension 0, may hold values from -500 to 500
- w_query: bfloat16 [128, 128], replicated, may hold values from -0.5 to 0.5
- w_key: bfloat16 [128, 128], replicated, may hold values from -0.5 to 0.5
- w_value: bfloat16 [128, 128], replicated, may hold values from -0.5 to 0.5
- w_gate: bfloat16 [128, 128], replicated, may hold values from -0.5 to 0.5
- w_out: bfloat16 [128, 128], replicated, may hold values from -0.5 to 0.5
- w_pair: bfloat16 [16, 4], replicated, may hold values from -1.5 to 1.5
- w_token: float32 [4], replicated, may hold values from -2 to 2
- offsets: int32 [320], P(('groups', 'atoms')), parts along dimension 0, may hold values from -128 to 32, as said below
- atom_token: int32 [10240], P(('groups', 'atoms')), parts along dimension 0, may hold values from 0 to 639, never falling along the last dimension, each value on 1 to 24 neighbouring positions
- padding: int32 [16], P(('groups', 'atoms')), parts along dimension 0, may hold values from 0 to 64, as said below
Outputs:
- grad_act: bfloat16 [16, 10240, 128], P('samples', ('groups', 'atoms')), parts along dimension 1
- grad_pair: bfloat16 [320, 32, 16, 128], P(('groups', 'atoms'), 'samples'), parts along dimension 0
- grad_weights: float32 [10, 128, 128], P('groups'), parts along dimension 0
- grad_pair_weight: float32 [32, 4], P('groups'), parts along dimension 0
- grad_token_weight: float32 [8], P('groups'), parts along dimension 0
The draws below stay inside these ranges and needn't reach their ends.
There are 2 independent parts, one for each index of `groups`. The reference program is written for one: setup_inputs(seed, part) draws one part's arguments, and reference() takes and returns one part's arrays. A program takes and returns all parts, laid end to end along the dimension named above; an argument that names none is the same for every part. Nothing has to cross between parts.
Inputs may be any that keep to these rules, and one draw needn't show every extreme that they name: Window w reads the 128 atoms that begin at 32 * w + offsets[w], moved into the complex. padding[r] atoms at the end of atom range r are padding. `atom_token`: the atoms of one token are contiguous, at most 24 of them.
All inputs are finite; a program needn't handle non-finite values.
Results may differ from the reference program's by a relative error of at most 0.025.
Values may be sent and summed in bfloat16 or wider, within the bound.
No kernel may reach another device: no remote copies, remote signals or barrier semaphores. Data moves between devices by JAX's collectives and lax.ppermute only.
A program may use at most 128 MiB of HBM per device.

```python
import math
import jax
import jax.numpy as jnp
import numpy as np
from jax import lax

C = 128
HEADS = 4
CP = 16
WQ = 32
WK = 128
ATOM_DEV = 640
NATOMS = 5120
SAMPLES = 16
NWIN = 160
NTOK = 640
RANGES = 8
PAD_MOST = 64


def draw_pair(key, part):
    full_shape = (NWIN, WQ, CP, WK)
    key_one = jax.random.fold_in(key, 0)
    return jnp.clip(jax.random.normal(key_one, full_shape, jnp.float32), -6.0, 6.0).astype(jnp.bfloat16)


def draw_offsets(key, part):
    values = jax.random.randint(key, (NWIN,), -WK, WQ + 1, dtype=jnp.int32)
    middle = NWIN // 2
    return values.at[middle].set(-WK).at[middle + 1].set(WQ)


def draw_padding(key, part):
    values = jax.random.randint(key, (RANGES,), 0, PAD_MOST + 1, dtype=jnp.int32)
    return values.at[0].set(PAD_MOST).at[RANGES - 1].set(0)


def level_of(key, shape, shards, low, high):
    def one(axis_at, shards_of):
        heights = jax.random.uniform(jax.random.fold_in(jax.random.fold_in(key, 6), axis_at), (shards_of,), jnp.float32, low / len(shards), high / len(shards))
        return jnp.repeat(jnp.exp(heights), shape[axis_at] // shards_of).reshape((-1,) + (1,) * (len(shape) - axis_at - 1))

    level = one(*shards[0])
    for cut in shards[1:]:
        level = level * one(*cut)
    return level


def profile(number_of, total, limit, slope):
    portions = [(1 << 20) // math.isqrt(rank ** slope) + 1 for rank in range(2, number_of + 1)]
    surplus, counts = total - limit - (number_of - 1), [1] * (number_of - 1)
    while surplus > 0:
        movable = [i for i in range(number_of - 1) if counts[i] < limit]
        whole, remaining = sum([portions[i] for i in movable]), surplus
        for i in movable:
            addition = min(limit - counts[i], max(1, remaining * portions[i] // whole), surplus)
            counts[i] = counts[i] + addition
            surplus = surplus - addition
    return np.array([limit] + counts)


def uneven(key, number_of, total, most, skew):
    if number_of == 2:
        one = jax.random.randint(key, (), max(1, total - most), min(most, total - 1) + 1)
        return jnp.stack([one, total - one])
    tallies = jnp.asarray(profile(number_of, total, most, skew), jnp.int32)
    pairs = (number_of - 1) // 2
    donor, receiver = tallies[1:1 + 2 * pairs:2], tallies[2:2 + 2 * pairs:2]
    slack = jnp.minimum(donor - 1, most - receiver)
    passed = jax.random.randint(jax.random.fold_in(key, 1), (pairs,), 0, 1 << 20) % (slack + 1)
    tallies = tallies.at[1:1 + 2 * pairs:2].set(donor - passed).at[2:2 + 2 * pairs:2].set(receiver + passed)
    return tallies[jax.random.permutation(jax.random.fold_in(key, 2), number_of)]


def normal_values(key, extent, scale, limit, cuts=(), kind=jnp.bfloat16):
    result = jax.random.normal(key, extent, jnp.float32) * scale
    if len(cuts) > 0:
        result = level_of(key, extent, cuts, -0.22, 0.18) * result
    return jnp.clip(result, min=-limit, max=limit).astype(kind)


def setup_inputs(seed: int = 0, part: int = 0) -> dict:
    arg_keys = jax.random.split(jax.random.key(seed), 14)
    part_keys = jax.random.split(jax.random.fold_in(arg_keys[13], part), 14)
    act = normal_values(part_keys[0], (SAMPLES, NATOMS, C), 1.0, 6.0, ((0, 2), (1, 8)))
    grad_out = normal_values(part_keys[1], (SAMPLES, NATOMS, C), 1.0, 6.0, ((0, 2), (1, 8)))
    pair = draw_pair(jax.random.fold_in(jax.random.fold_in(arg_keys[13], part), 71), part)
    w_query = normal_values(arg_keys[3], (C, C), C ** -0.5, 0.5)
    w_key = normal_values(arg_keys[4], (C, C), C ** -0.5, 0.5)
    w_value = normal_values(arg_keys[5], (C, C), C ** -0.5, 0.5)
    w_gate = normal_values(arg_keys[6], (C, C), C ** -0.5, 0.5)
    w_out = normal_values(arg_keys[7], (C, C), C ** -0.5, 0.5)
    w_pair = normal_values(arg_keys[8], (CP, HEADS), CP ** -0.5, 1.5)
    w_token = jnp.clip(jax.random.uniform(arg_keys[9], (HEADS,), jnp.float32, -2.0, 2.0), -2.0, 2.0)
    offsets = draw_offsets(jax.random.fold_in(jax.random.fold_in(arg_keys[13], part), 71), part)
    atom_token = jnp.searchsorted(jnp.cumsum(uneven(part_keys[11], NTOK, NATOMS, 24, 2)), jnp.arange(NATOMS), side="right").astype(jnp.int32)
    padding = draw_padding(jax.random.fold_in(jax.random.fold_in(arg_keys[13], part), 71), part)
    return {"act": act, "grad_out": grad_out, "pair": pair, "w_query": w_query, "w_key": w_key, "w_value": w_value, "w_gate": w_gate, "w_out": w_out, "w_pair": w_pair, "w_token": w_token, "offsets": offsets, "atom_token": atom_token, "padding": padding}


MASKED = -1000000000.0

def float_einsum(pattern, left_op, right_op):
    return jnp.einsum(pattern, left_op.astype(jnp.float32), right_op.astype(jnp.float32), precision=lax.Precision.HIGHEST)

def window_layout(offsets, atom_token, padding):
    position = jnp.arange(NATOMS, dtype=jnp.int32)
    ranges = (position // ATOM_DEV).astype(jnp.int32)
    is_live = position % ATOM_DEV < ATOM_DEV - padding[ranges]
    starts = jnp.clip(WQ * jnp.arange(NWIN, dtype=jnp.int32) + offsets, 0, NATOMS - WK).astype(jnp.int32)
    key_rows = (starts[:, None] + jnp.arange(WK, dtype=jnp.int32)[None, :]).astype(jnp.int32)
    key_live = is_live[key_rows]
    same_token = atom_token.reshape(NWIN, WQ)[:, :, None] == atom_token[key_rows][:, None, :]
    return (key_rows, key_live, same_token)

def attend(query, keys, values, gate_logit, grad_y, pair_bias, key_live):
    windows = keys.shape[0]
    head_count = pair_bias.shape[1]
    channels = query.shape[-1]
    head_dim = channels // head_count
    score_scale = 1.0 / math.sqrt(head_dim)
    query_heads = query.reshape(windows, -1, head_count, head_dim)
    key_heads = keys.reshape(windows, -1, head_count, head_dim)
    value_heads = values.reshape(windows, -1, head_count, head_dim)
    scores = float_einsum('wihd,wjhd->whij', query_heads, key_heads) * score_scale + pair_bias
    scores = jnp.where(key_live[:, None, None, :], scores, MASKED)
    row_max = lax.optimization_barrier(jnp.max(scores, axis=-1, keepdims=True))
    exponent = jnp.exp(scores - row_max)
    attn_probs = exponent / lax.optimization_barrier(jnp.sum(exponent, axis=-1, keepdims=True))
    probs_b = attn_probs.astype(jnp.bfloat16)
    attended = float_einsum('whij,wjhd->wihd', probs_b, value_heads).reshape(query.shape)
    gate_value = jax.nn.sigmoid(gate_logit)
    gated = (gate_value * attended).astype(jnp.bfloat16)
    d_attended = (grad_y * gate_value).astype(jnp.bfloat16)
    d_gate = (grad_y * attended * gate_value * (1.0 - gate_value)).astype(jnp.bfloat16)
    attended_heads = d_attended.reshape(windows, -1, head_count, head_dim)
    d_probs = float_einsum('wihd,wjhd->whij', attended_heads, value_heads)
    d_scores = attn_probs * (d_probs - lax.optimization_barrier(jnp.sum(attn_probs * d_probs, axis=-1, keepdims=True)))
    ds_b = d_scores.astype(jnp.bfloat16)
    d_query = (float_einsum('whij,wjhd->wihd', ds_b, key_heads) * score_scale).astype(jnp.bfloat16).reshape(query.shape)
    d_keys = float_einsum('whij,wihd->wjhd', ds_b, query_heads) * score_scale
    d_values = float_einsum('whij,wihd->wjhd', probs_b, attended_heads)
    return (gated, d_query, d_gate, d_keys, d_values, d_scores)

def reference(act, grad_out, pair, w_query, w_key, w_value, w_gate, w_out, w_pair, w_token, offsets, atom_token, padding):
    key_rows, key_live, same_token = window_layout(offsets, atom_token, padding)
    same_float = same_token.astype(jnp.float32)
    pair_bias = float_einsum('wicj,ch->whij', pair, w_pair) + w_token[None, :, None, None] * same_float[:, None, :, :]
    projection = jnp.concatenate([w_query, w_key, w_value, w_gate], axis=1)

    def one_sample(running, inputs):
        bias_sum, weight_sum, out_sum = running
        sample_act, sample_grad = inputs
        mixed = jnp.dot(sample_act, projection, preferred_element_type=jnp.float32)
        query = mixed[:, :C].astype(jnp.bfloat16)
        keys = mixed[:, C:2 * C].astype(jnp.bfloat16)
        values = mixed[:, 2 * C:3 * C].astype(jnp.bfloat16)
        gate_logit = mixed[:, 3 * C:]
        grad_y = jnp.dot(sample_grad, w_out.T, preferred_element_type=jnp.float32)
        gated, d_query, d_gate, d_keys, d_values, d_scores = attend(query, keys[key_rows], values[key_rows], gate_logit, grad_y, pair_bias, key_live)
        key_grad = jnp.zeros((NATOMS, C), jnp.float32).at[key_rows].add(d_keys.reshape(NWIN, WK, C))
        value_grad = jnp.zeros((NATOMS, C), jnp.float32).at[key_rows].add(d_values.reshape(NWIN, WK, C))
        stacked = jnp.concatenate([d_query, key_grad.astype(jnp.bfloat16), value_grad.astype(jnp.bfloat16), d_gate], axis=1)
        grad_act = jnp.dot(stacked, projection.T, preferred_element_type=jnp.float32).astype(jnp.bfloat16)
        weight_sum = weight_sum + jnp.dot(sample_act.T, stacked, preferred_element_type=jnp.float32)
        out_sum = out_sum + jnp.dot(gated.T, sample_grad, preferred_element_type=jnp.float32)
        return ((bias_sum + d_scores, weight_sum, out_sum), grad_act)
    start_state = (jnp.zeros((NWIN, HEADS, WQ, WK), jnp.float32), jnp.zeros((C, 4 * C), jnp.float32), jnp.zeros((C, C), jnp.float32))
    (bias_total, weight_sum, out_sum), grad_act = lax.scan(one_sample, start_state, (act, grad_out))
    grad_pair = float_einsum('whij,ch->wicj', bias_total, w_pair).astype(jnp.bfloat16)
    grad_weights = jnp.concatenate([weight_sum.reshape(C, 4, C).transpose(1, 0, 2), out_sum[None]], axis=0)
    grad_pair_weight = float_einsum('wicj,whij->ch', pair, bias_total)
    grad_token_weight = lax.optimization_barrier(jnp.sum(bias_total * same_float[:, None, :, :], axis=(0, 2, 3)))
    return (grad_act, grad_pair, grad_weights, grad_pair_weight, grad_token_weight)
```

```python
import functools
import math

import jax
import jax.numpy as jnp
from jax import lax
from jax.experimental import pallas as pl
from jax.experimental.pallas import tpu as pltpu
from jax.sharding import PartitionSpec as P

BF16 = jnp.bfloat16
F32 = jnp.float32
MASKED = -1000000000.0
LOG2E = math.log2(math.e)
CODE_ROWS = 16
CODE_BASE = 128
SMALL_ROWS = 16
VMEM_LIMIT = 56 * 1024 * 1024


def dot(a, b):
    return lax.dot_general(a, b, (((1,), (0,)), ((), ())), preferred_element_type=F32)


def dot_nt(a, b):
    return lax.dot_general(a, b, (((1,), (1,)), ((), ())), preferred_element_type=F32)


def dot_tn(a, b):
    return lax.dot_general(a, b, (((0,), (0,)), ((), ())), preferred_element_type=F32)


def column_of(row, span):
    return jnp.broadcast_to(row, (span, row.shape[-1])).T


class Side:
    def __init__(self, windows, query_row, rows, pieces, origin):
        self.windows = windows
        self.query_row = query_row
        self.rows = rows
        self.pieces = pieces
        self.origin = origin


def attention_kernel(geo, sides, edge, *refs):
    samples, atoms, channels, heads, win_rows, span, cp, out_half = geo
    refs = list(refs)
    take = lambda n: [refs.pop(0) for _ in range(n)]
    meta_ref, wtok_ref = take(2)
    act_ref, gout_ref, codes_ref, qcode_ref, pair_hbm = take(5)
    wq_ref, wk_ref, wv_ref, wg_ref, wo_ref, wpair_ref = take(6)
    if edge:
        lo_ref, hi_ref, ga_in_ref, acc_in_ref = take(4)
        ga_ref, ga_lo_ref, ga_hi_ref, acc_ref, mine_ref, other_ref = take(6)
    else:
        ga_ref, acc_ref, mine_ref, other_ref = take(4)
    pair_ref, pair_sem, wexp_ref, pw_ref, code_ref, q_ref, datt_ref, g_ref, gy_ref = take(9)
    dq_ref, dgate_ref, gated_ref, bias_ref, bsum_ref = take(5)
    n_blocks = len(sides) * samples
    k_refs = take(n_blocks)
    v_refs = take(n_blocks)
    dk_refs = take(n_blocks)
    dv_refs = take(n_blocks)

    half_rows = win_rows // 2
    head_dim = channels // heads
    scale = 1.0 / math.sqrt(head_dim)
    halo = {"lo": None, "hi": None}
    if edge:
        halo = {"lo": lo_ref, "hi": hi_ref}

    copies = []
    first = 0
    for n, side in enumerate(sides):
        count = len(side.windows)
        copies.append(
            pltpu.make_async_copy(
                pair_hbm.at[pl.ds(side.windows[0], count)],
                pair_ref.at[pl.ds(first, count)],
                pair_sem.at[n],
            )
        )
        first += count
    for copy in copies:
        copy.start()

    def act_piece(source, row, rows, s):
        if source == "act":
            return act_ref[s, row : row + rows, :]
        return halo[source][s * span : s * span + rows, :]

    lane = lax.broadcasted_iota(jnp.int32, (1, channels), 1)
    head_masks = [(lane // head_dim == h).astype(F32) for h in range(heads)]
    head_masks_b = [m.astype(BF16) for m in head_masks]

    lanes = 2 * heads * half_rows
    s_lane = lax.broadcasted_iota(jnp.int32, (1, lanes), 1)
    lane_head = (s_lane // half_rows) % heads
    lane_row = (s_lane // (heads * half_rows)) * half_rows + s_lane % half_rows
    wtok = jnp.zeros((1, lanes), F32)
    for h in range(heads):
        wtok = jnp.where(lane_head == h, wtok_ref[h], wtok)
    pick = (
        lax.broadcasted_iota(jnp.int32, (heads, lanes), 0)
        == (lax.broadcasted_iota(jnp.int32, (heads, lanes), 1) // half_rows) % heads
    ).astype(BF16)
    wlane = dot(wpair_ref[...], pick).astype(BF16)
    for i in range(win_rows):
        wexp_ref[i * cp : (i + 1) * cp, :] = jnp.where(lane_row == i, wlane, 0.0).astype(BF16)
    pw_ref[...] = jnp.zeros_like(pw_ref)

    for n, side in enumerate(sides):
        for source, row, rows, at in side.pieces:
            for r in range(0, rows, span):
                if source == "act":
                    code_row = codes_ref[:, row + r : row + r + span]
                else:
                    two = halo[source][samples * span : samples * span + CODE_ROWS, :].astype(F32)
                    code_row = two[0:1, :] * CODE_BASE + two[1:2, :]
                code_ref[n, at + r : at + r + span, :] = column_of(code_row, span)

    w_kv = jnp.concatenate([wk_ref[...], wv_ref[...]], axis=1)
    w_qg = jnp.concatenate([wq_ref[...], wg_ref[...]], axis=1)
    for n, side in enumerate(sides):
        queries = len(side.windows) * win_rows
        for s in range(samples):
            block = n * samples + s
            for source, row, rows, at in side.pieces:
                kv = dot(act_piece(source, row, rows, s), w_kv)
                k_refs[block][at : at + rows, :] = kv[:, :channels]
                v_refs[block][at : at + rows, :] = kv[:, channels:]
            dk_refs[block][...] = jnp.zeros_like(dk_refs[block])
            dv_refs[block][...] = jnp.zeros_like(dv_refs[block])
            qrow = side.query_row
            qg = dot(act_ref[s, qrow : qrow + queries, :], w_qg)
            q_ref[block] = qg[:, :channels].astype(BF16)
            gate = jax.nn.sigmoid(qg[:, channels:])
            gy = dot_nt(gout_ref[s, qrow : qrow + queries, :], wo_ref[...])
            g_ref[block] = gate
            gy_ref[block] = gy
            datt_ref[block] = (gy * gate).astype(BF16)

    for copy in copies:
        copy.wait()

    def by_head(rows):
        return jnp.concatenate(
            [
                rows[half * half_rows : (half + 1) * half_rows] * head_masks_b[h]
                for half in range(2)
                for h in range(heads)
            ],
            axis=0,
        )

    def own_head(wide):
        halves = []
        for half in range(2):
            total = None
            for h in range(heads):
                at = (half * heads + h) * half_rows
                term = wide[at : at + half_rows] * head_masks[h]
                total = term if total is None else total + term
            halves.append(total)
        return jnp.concatenate(halves, axis=0)

    def one_window(n, side, first, w, tok_sum):
        slot = first + w
        start = meta_ref[side.windows[0] + w] - side.origin
        key_codes = code_ref[n, pl.ds(start, span), :]
        same = key_codes == qcode_ref[pl.ds(side.windows[0] + w, 1), :]
        pair_w = pair_ref[slot]
        bias = dot_tn(pair_w, wexp_ref[...]) + jnp.where(same, wtok, 0.0)
        bias_ref[...] = jnp.where(key_codes > 0.0, bias, MASKED) * LOG2E
        qrows = pl.ds(pl.multiple_of(w * win_rows, win_rows), win_rows)
        for s in range(samples):
            block = n * samples + s
            keys = pl.ds(start, span)
            kb = k_refs[block][keys, :].astype(BF16)
            vb = v_refs[block][keys, :].astype(BF16)
            qh = by_head(q_ref[block, qrows, :])
            dh = by_head(datt_ref[block, qrows, :])
            x = dot_nt(kb, qh) * (scale * LOG2E) + bias_ref[...]
            dp = dot_nt(vb, dh)
            e = jnp.exp2(x - jnp.max(x, axis=0, keepdims=True))
            p = e * (1.0 / jnp.sum(e, axis=0, keepdims=True))
            t = p * dp
            ds = t - p * jnp.sum(t, axis=0, keepdims=True)
            if s == 0:
                bsum_ref[...] = ds
            else:
                bsum_ref[...] += ds
            pb = p.astype(BF16)
            dsb = ds.astype(BF16)
            dk_refs[block][keys, :] += dot(dsb, qh)
            dv_refs[block][keys, :] += dot(pb, dh)
            att = own_head(dot_tn(pb, vb))
            dq_ref[block, qrows, :] = (own_head(dot_tn(dsb, kb)) * scale).astype(BF16)
            gate = g_ref[block, qrows, :]
            ga = gate * att
            gated_ref[block, qrows, :] = ga.astype(BF16)
            dgate_ref[block, qrows, :] = (gy_ref[block, qrows, :] * ga * (1.0 - gate)).astype(BF16)
        total = bsum_ref[...]
        total_b = total.astype(BF16)
        pw_ref[...] += dot(pair_w, total_b)
        straight = total.T
        bsum_ref[...] = straight
        core = meta_ref[meta_ref.shape[0] - 1]
        width = heads * half_rows
        mine_ref[slot] = bsum_ref[pl.ds(pl.multiple_of(core * width, width), width), :]
        other_ref[slot] = bsum_ref[
            pl.ds(pl.multiple_of((1 - core) * width, width), width), :
        ].astype(BF16)
        return tok_sum + jnp.sum(jnp.where(same, total, 0.0), axis=0, keepdims=True)

    tok_sum = jnp.zeros((1, lanes), F32)
    first = 0
    for n, side in enumerate(sides):
        count = len(side.windows)
        tok_sum = lax.fori_loop(
            0, count, functools.partial(one_window, n, side, first), tok_sum
        )
        first += count

    if edge:
        ga_ref[...] = ga_in_ref[...]
    acc_kv = jnp.zeros((channels, 2 * channels), F32)
    acc_qg = jnp.zeros((channels, 2 * channels), F32)
    acc_o = jnp.zeros((channels, channels), F32)
    for n, side in enumerate(sides):
        queries = len(side.windows) * win_rows
        qrow = side.query_row
        for s in range(samples):
            block = n * samples + s
            for source, row, rows, at in side.pieces:
                dk = dk_refs[block][at : at + rows, :] * scale
                dv = dv_refs[block][at : at + rows, :]
                dkv_b = jnp.concatenate([dk.astype(BF16), dv.astype(BF16)], axis=1)
                part = dot_nt(dkv_b, w_kv)
                if source == "lo":
                    ga_lo_ref[s] = part.astype(BF16)
                elif source == "hi":
                    ga_hi_ref[s] = part.astype(BF16)
                elif edge:
                    ga_ref[s, row : row + rows, :] += part
                else:
                    ga_ref[s, row : row + rows, :] = part
                acc_kv = acc_kv + dot_tn(act_piece(source, row, rows, s), dkv_b)
            dqg = jnp.concatenate([dq_ref[block], dgate_ref[block]], axis=1)
            ga_ref[s, qrow : qrow + queries, :] += dot_nt(dqg, w_qg)
            acc_qg = acc_qg + dot_tn(act_ref[s, qrow : qrow + queries, :], dqg)
            acc_o = acc_o + dot_tn(gated_ref[block], gout_ref[s, qrow : qrow + queries, :])

    diag = lax.broadcasted_iota(jnp.int32, (win_rows * cp, lanes), 0) // cp == lane_row
    pw = jnp.where(diag, pw_ref[...], 0.0).reshape(win_rows, cp, lanes).sum(axis=0)
    parts = [
        acc_qg[:, :channels],
        acc_kv[:, :channels],
        acc_kv[:, channels:],
        acc_qg[:, channels:],
        acc_o,
    ]
    first_half, second_half = [], []
    left = out_half
    for part in parts:
        if left >= channels:
            first_half.append(part)
            left -= channels
        elif left > 0:
            first_half.append(part[:left])
            second_half.append(part[left:])
            left = 0
        else:
            second_half.append(part)
    tok_rows = jnp.where(
        lax.broadcasted_iota(jnp.int32, (SMALL_ROWS, lanes), 0) == 0, tok_sum, 0.0
    )
    at = 0
    for part in first_half + [pw] + second_half + [tok_rows]:
        rows = part.shape[0]
        if edge:
            acc_ref[at : at + rows, :] = part + acc_in_ref[at : at + rows, :]
        else:
            acc_ref[at : at + rows, :] = part
        at += rows


def pair_kernel(wpair_ref, m1_ref, r1_ref, m2_ref, r2_ref, out_ref, *, order, heads, cp):
    rows = m1_ref.shape[1]
    half_rows = rows // heads
    lane = lax.broadcasted_iota(jnp.int32, (1, rows), 1)
    pick = (
        lax.broadcasted_iota(jnp.int32, (heads, rows), 0)
        == lax.broadcasted_iota(jnp.int32, (heads, rows), 1) // half_rows
    ).astype(BF16)
    wlane = dot(wpair_ref[...], pick)
    wexp = jnp.concatenate(
        [jnp.where(lane % half_rows == i, wlane, 0.0) for i in range(half_rows)], axis=0
    ).astype(BF16)
    for which, (m_ref, r_ref) in enumerate(((m1_ref, r1_ref), (m2_ref, r2_ref))):
        for slot, window in enumerate(order[which]):
            total = (m_ref[slot] + r_ref[slot].astype(F32)).astype(BF16)
            out_ref[window] = dot(wexp, total).astype(BF16)


def per_device(
    act,
    grad_out,
    pair,
    w_query,
    w_key,
    w_value,
    w_gate,
    w_out,
    w_pair,
    w_token,
    offsets,
    atom_token,
    padding,
):
    samples, atoms, channels = act.shape
    windows = offsets.shape[0]
    win_rows = atoms // windows
    span = pair.shape[-1]
    cp, heads = w_pair.shape
    half_rows = win_rows // 2
    lanes = heads * win_rows
    ranges = lax.axis_size("atoms")
    cores = lax.axis_size("samples")
    assert cores == 2 and ranges & (ranges - 1) == 0
    core = lax.axis_index("samples")
    anchor = lax.axis_index("atoms") * atoms
    position = jnp.arange(atoms, dtype=jnp.int32)
    codes = jnp.where(position < atoms - padding[0], atom_token + 1, 0)
    starts = (
        jnp.clip(
            anchor + win_rows * jnp.arange(windows, dtype=jnp.int32) + offsets,
            0,
            ranges * atoms - span,
        )
        - anchor
    )
    edge_count = span // win_rows
    inner = tuple(range(edge_count, windows - edge_count))
    low, high = tuple(range(edge_count)), tuple(range(windows - edge_count, windows))
    own = edge_count * win_rows + span
    edge_rows = own + span
    index = jnp.arange(windows, dtype=jnp.int32)
    low_limit = jnp.where(
        index < edge_count, -span, jnp.where(index < windows - edge_count, 0, atoms - own)
    )
    high_limit = jnp.where(
        index < edge_count,
        own - span,
        jnp.where(index < windows - edge_count, atoms - span, atoms),
    )
    starts = jnp.clip(starts, low_limit, high_limit)
    meta = jnp.concatenate([starts, core[None].astype(jnp.int32)])
    qcode = jnp.broadcast_to(
        (atom_token + 1).astype(F32).reshape(windows, 2, 1, half_rows),
        (windows, 2, heads, half_rows),
    ).reshape(windows, lanes)
    codes_f = codes.astype(F32).reshape(1, atoms)

    def payload(first):
        part = lax.slice_in_dim(act, first, first + span, axis=1).reshape(-1, channels)
        code = lax.slice_in_dim(codes, first, first + span)[None]
        extra = jnp.concatenate(
            [code // CODE_BASE, code % CODE_BASE, jnp.zeros((CODE_ROWS - 2, span), jnp.int32)]
        )
        return jnp.concatenate([part, extra.astype(BF16)])

    up = [(i, i + 1) for i in range(ranges - 1)]
    down = [(j, i) for i, j in up]
    halo_lo = lax.ppermute(payload(atoms - span), "atoms", up)
    halo_hi = lax.ppermute(payload(0), "atoms", down)

    out_half = 5 * channels // 2
    acc_rows = 5 * channels + 2 * SMALL_ROWS
    geo = (samples, atoms, channels, heads, win_rows, span, cp, out_half)
    pair_flat = pair.reshape(windows, win_rows * cp, span)
    vmem = pl.BlockSpec(memory_space=pltpu.VMEM)
    smem = pl.BlockSpec(memory_space=pltpu.SMEM)
    hbm = pl.BlockSpec(memory_space=pl.ANY)
    width = heads * half_rows

    def call(sides, edge, args):
        count = sum(len(side.windows) for side in sides)
        queries = len(sides[0].windows) * win_rows
        rows = sides[0].rows
        blocks = len(sides) * samples
        out_shape = [jax.ShapeDtypeStruct((samples, atoms, channels), F32)]
        if edge:
            out_shape += [jax.ShapeDtypeStruct((samples, span, channels), BF16)] * 2
        out_shape += [
            jax.ShapeDtypeStruct((acc_rows, channels), F32),
            jax.ShapeDtypeStruct((count, width, span), F32),
            jax.ShapeDtypeStruct((count, width, span), BF16),
        ]
        per_query = (blocks, queries, channels)
        scratch = [
            pltpu.VMEM((count, win_rows * cp, span), BF16),
            pltpu.SemaphoreType.DMA((len(sides),)),
            pltpu.VMEM((win_rows * cp, lanes), BF16),
            pltpu.VMEM((win_rows * cp, lanes), F32),
            pltpu.VMEM((len(sides), rows, span), F32),
            pltpu.VMEM(per_query, BF16),
            pltpu.VMEM(per_query, BF16),
            pltpu.VMEM(per_query, F32),
            pltpu.VMEM(per_query, F32),
            pltpu.VMEM(per_query, BF16),
            pltpu.VMEM(per_query, BF16),
            pltpu.VMEM(per_query, BF16),
            pltpu.VMEM((span, lanes), F32),
            pltpu.VMEM((span, lanes), F32),
        ]
        scratch += [pltpu.VMEM((rows, channels), F32)] * (4 * blocks)
        units = 6 * count * samples + 8 * count + 14 * blocks
        return pl.pallas_call(
            functools.partial(attention_kernel, geo, sides, edge),
            out_shape=out_shape,
            in_specs=[smem] * 2 + [vmem] * 4 + [hbm] + [vmem] * (len(args) - 7),
            out_specs=[vmem] * len(out_shape),
            scratch_shapes=scratch,
            compiler_params=pltpu.CompilerParams(vmem_limit_bytes=VMEM_LIMIT),
            cost_estimate=pl.CostEstimate(
                flops=2 * units * 128 * 128 * 128 * 4,
                bytes_accessed=12_000_000,
                transcendentals=count * samples * span * lanes,
            ),
        )(*args)

    common = (
        meta,
        w_token,
        act,
        grad_out,
        codes_f,
        qcode,
        pair_flat,
        w_query,
        w_key,
        w_value,
        w_gate,
        w_out,
        w_pair,
    )
    inner_side = Side(inner, span, atoms, [("act", 0, atoms, 0)], 0)
    ga1, acc1, mine1, other1 = call([inner_side], False, common)
    swap = [(0, 1), (1, 0)]
    recv1 = lax.ppermute(other1, "samples", swap)

    low_side = Side(low, 0, edge_rows, [("lo", 0, span, 0), ("act", 0, own, span)], -span)
    high_side = Side(
        high,
        atoms - span,
        edge_rows,
        [("act", atoms - own, own, 0), ("hi", 0, span, own)],
        atoms - own,
    )
    ga2, ga_lo, ga_hi, acc, mine2, other2 = call(
        [low_side, high_side], True, common + (halo_lo, halo_hi, ga1, acc1)
    )
    recv2 = lax.ppermute(other2, "samples", swap)
    from_upper = lax.ppermute(ga_lo, "atoms", down)
    from_lower = lax.ppermute(ga_hi, "atoms", up)

    part_rows = acc_rows // 2
    wide = part_rows - SMALL_ROWS

    def encode(value):
        big, small = value[:wide].astype(BF16), value[wide:]
        top = small.astype(BF16)
        return jnp.concatenate([big, top, (small - top.astype(F32)).astype(BF16)])

    def decode(sent):
        sent = sent.astype(F32)
        return jnp.concatenate(
            [sent[:wide], sent[wide : wide + SMALL_ROWS] + sent[wide + SMALL_ROWS :]]
        )

    acc = acc.reshape(2, part_rows, channels)
    mine = encode(lax.dynamic_index_in_dim(acc, core, 0, keepdims=False))
    other = encode(lax.dynamic_index_in_dim(acc, 1 - core, 0, keepdims=False))
    total = decode(mine) + decode(lax.ppermute(other, "samples", swap))
    step = 1
    while step < ranges:
        sent = encode(total)
        got = lax.ppermute(sent, "atoms", [(i, i ^ step) for i in range(ranges)])
        total = decode(sent) + decode(got)
        step *= 2
    sent = encode(total)
    got = lax.ppermute(sent, "samples", swap)
    is_first = core == 0
    first = decode(jnp.where(is_first, sent, got))
    second = decode(jnp.where(is_first, got, sent))
    grad_weights = jnp.concatenate([first[:wide], second[:wide]]).reshape(5, channels, channels)
    grad_pair_weight = first[wide:].reshape(cp, 2, heads, half_rows).sum(axis=(1, 3))
    grad_token_weight = second[wide].reshape(2, heads, half_rows).sum(axis=(0, 2))

    grad_pair = pl.pallas_call(
        functools.partial(pair_kernel, order=(inner, low + high), heads=heads, cp=cp),
        out_shape=jax.ShapeDtypeStruct((windows, half_rows * cp, span), BF16),
        in_specs=[vmem] * 5,
        out_specs=vmem,
        compiler_params=pltpu.CompilerParams(vmem_limit_bytes=VMEM_LIMIT),
        cost_estimate=pl.CostEstimate(
            flops=2 * windows * 256 * 256 * 256, bytes_accessed=4_000_000, transcendentals=0
        ),
    )(w_pair, mine1, recv1, mine2, recv2).reshape(windows, half_rows, cp, span)

    grad_act = (
        ga2.at[:, :span]
        .add(from_lower.astype(F32))
        .at[:, atoms - span :]
        .add(from_upper.astype(F32))
        .astype(BF16)
    )
    return (grad_act, grad_pair, grad_weights, grad_pair_weight, grad_token_weight)


def solution(mesh):
    in_specs = (
        P("samples", ("groups", "atoms"), None),
        P("samples", ("groups", "atoms"), None),
        P(("groups", "atoms"), None, None, None),
        P(),
        P(),
        P(),
        P(),
        P(),
        P(),
        P(),
        P(("groups", "atoms")),
        P(("groups", "atoms")),
        P(("groups", "atoms")),
    )
    out_specs = (
        P("samples", ("groups", "atoms"), None),
        P(("groups", "atoms"), "samples", None, None),
        P("groups", None, None),
        P("groups", None),
        P("groups"),
    )
    return jax.shard_map(
        per_device, mesh=mesh, in_specs=in_specs, out_specs=out_specs, check_vma=False
    )
```

```python
import functools
import math

import jax
import jax.numpy as jnp
from jax import lax
from jax.experimental import pallas as pl
from jax.experimental.pallas import tpu as pltpu
from jax.sharding import PartitionSpec as P

BF16 = jnp.bfloat16
F32 = jnp.float32
MASKED = -1000000000.0
LOG2E = math.log2(math.e)
CODE_ROWS = 16
CODE_BASE = 128
SMALL_ROWS = 16
VMEM_LIMIT = 56 * 1024 * 1024


def dot(a, b):
    return lax.dot_general(a, b, (((1,), (0,)), ((), ())), preferred_element_type=F32)


def dot_nt(a, b):
    return lax.dot_general(a, b, (((1,), (1,)), ((), ())), preferred_element_type=F32)


def dot_tn(a, b):
    return lax.dot_general(a, b, (((0,), (0,)), ((), ())), preferred_element_type=F32)


def column_of(row, span):
    return jnp.broadcast_to(row, (span, row.shape[-1])).T


class Side:
    def __init__(self, windows, query_row, rows, pieces, origin):
        self.windows = windows
        self.query_row = query_row
        self.rows = rows
        self.pieces = pieces
        self.origin = origin


def attention_kernel(geo, sides, edge, *refs):
    samples, atoms, channels, heads, win_rows, span, cp, out_half = geo
    refs = list(refs)
    take = lambda n: [refs.pop(0) for _ in range(n)]
    meta_ref, wtok_ref = take(2)
    act_ref, gout_ref, codes_ref, qcode_ref, pair_hbm = take(5)
    wq_ref, wk_ref, wv_ref, wg_ref, wo_ref, wpair_ref = take(6)
    if edge:
        lo_ref, hi_ref, ga_in_ref, acc_in_ref = take(4)
        ga_ref, ga_lo_ref, ga_hi_ref, acc_ref, mine_ref, other_ref = take(6)
    else:
        ga_ref, acc_ref, mine_ref, other_ref = take(4)
    pair_ref, pair_sem, wexp_ref, pw_ref, code_ref, q_ref, datt_ref, g_ref, gy_ref = take(9)
    dq_ref, dgate_ref, gated_ref, bias_ref, bsum_ref = take(5)
    n_blocks = len(sides) * samples
    k_refs = take(n_blocks)
    v_refs = take(n_blocks)
    dk_refs = take(n_blocks)
    dv_refs = take(n_blocks)

    half_rows = win_rows // 2
    head_dim = channels // heads
    scale = 1.0 / math.sqrt(head_dim)
    halo = {"lo": None, "hi": None}
    if edge:
        halo = {"lo": lo_ref, "hi": hi_ref}

    copies = []
    first = 0
    for n, side in enumerate(sides):
        count = len(side.windows)
        copies.append(
            pltpu.make_async_copy(
                pair_hbm.at[pl.ds(side.windows[0], count)],
                pair_ref.at[pl.ds(first, count)],
                pair_sem.at[n],
            )
        )
        first += count
    for copy in copies:
        copy.start()

    def act_piece(source, row, rows, s):
        if source == "act":
            return act_ref[s, row : row + rows, :]
        return halo[source][s * span : s * span + rows, :]

    lane = lax.broadcasted_iota(jnp.int32, (1, channels), 1)
    head_masks = [(lane // head_dim == h).astype(F32) for h in range(heads)]
    head_masks_b = [m.astype(BF16) for m in head_masks]

    lanes = 2 * heads * half_rows
    s_lane = lax.broadcasted_iota(jnp.int32, (1, lanes), 1)
    lane_head = (s_lane // half_rows) % heads
    lane_row = (s_lane // (heads * half_rows)) * half_rows + s_lane % half_rows
    wtok = jnp.zeros((1, lanes), F32)
    for h in range(heads):
        wtok = jnp.where(lane_head == h, wtok_ref[h], wtok)
    pick = (
        lax.broadcasted_iota(jnp.int32, (heads, lanes), 0)
        == (lax.broadcasted_iota(jnp.int32, (heads, lanes), 1) // half_rows) % heads
    ).astype(BF16)
    wlane = dot(wpair_ref[...], pick).astype(BF16)
    for i in range(win_rows):
        wexp_ref[i * cp : (i + 1) * cp, :] = jnp.where(lane_row == i, wlane, 0.0).astype(BF16)
    pw_ref[...] = jnp.zeros_like(pw_ref)

    for n, side in enumerate(sides):
        for source, row, rows, at in side.pieces:
            for r in range(0, rows, span):
                if source == "act":
                    code_row = codes_ref[:, row + r : row + r + span]
                else:
                    two = halo[source][samples * span : samples * span + CODE_ROWS, :].astype(F32)
                    code_row = two[0:1, :] * CODE_BASE + two[1:2, :]
                code_ref[n, at + r : at + r + span, :] = column_of(code_row, span)

    w_kv = jnp.concatenate([wk_ref[...], wv_ref[...]], axis=1)
    w_qg = jnp.concatenate([wq_ref[...], wg_ref[...]], axis=1)
    for n, side in enumerate(sides):
        queries = len(side.windows) * win_rows
        for s in range(samples):
            block = n * samples + s
            for source, row, rows, at in side.pieces:
                kv = dot(act_piece(source, row, rows, s), w_kv)
                k_refs[block][at : at + rows, :] = kv[:, :channels]
                v_refs[block][at : at + rows, :] = kv[:, channels:]
            dk_refs[block][...] = jnp.zeros_like(dk_refs[block])
            dv_refs[block][...] = jnp.zeros_like(dv_refs[block])
            qrow = side.query_row
            qg = dot(act_ref[s, qrow : qrow + queries, :], w_qg)
            q_ref[block] = qg[:, :channels].astype(BF16)
            gate = jax.nn.sigmoid(qg[:, channels:])
            gy = dot_nt(gout_ref[s, qrow : qrow + queries, :], wo_ref[...])
            g_ref[block] = gate
            gy_ref[block] = gy
            datt_ref[block] = (gy * gate).astype(BF16)

    for copy in copies:
        copy.wait()

    def by_head(rows):
        return jnp.concatenate(
            [
                rows[half * half_rows : (half + 1) * half_rows] * head_masks_b[h]
                for half in range(2)
                for h in range(heads)
            ],
            axis=0,
        )

    def own_head(wide):
        halves = []
        for half in range(2):
            total = None
            for h in range(heads):
                at = (half * heads + h) * half_rows
                term = wide[at : at + half_rows] * head_masks[h]
                total = term if total is None else total + term
            halves.append(total)
        return jnp.concatenate(halves, axis=0)

    def one_window(n, side, first, w, tok_sum):
        slot = first + w
        start = meta_ref[side.windows[0] + w] - side.origin
        key_codes = code_ref[n, pl.ds(start, span), :]
        same = key_codes == qcode_ref[pl.ds(side.windows[0] + w, 1), :]
        pair_w = pair_ref[slot]
        bias = dot_tn(pair_w, wexp_ref[...]) + jnp.where(same, wtok, 0.0)
        bias_ref[...] = jnp.where(key_codes > 0.0, bias, MASKED) * LOG2E
        qrows = pl.ds(pl.multiple_of(w * win_rows, win_rows), win_rows)
        keys = pl.ds(start, span)

        def products(s):
            block = n * samples + s
            kb = k_refs[block][keys, :].astype(BF16)
            vb = v_refs[block][keys, :].astype(BF16)
            qh = by_head(q_ref[block, qrows, :])
            dh = by_head(datt_ref[block, qrows, :])
            return block, kb, vb, qh, dh, dot_nt(kb, qh), dot_nt(vb, dh)

        def softmax(state):
            block, kb, vb, qh, dh, x, dp = state
            x = x * (scale * LOG2E) + bias_ref[...]
            e = jnp.exp2(x - jnp.max(x, axis=0, keepdims=True))
            p = e * (1.0 / jnp.sum(e, axis=0, keepdims=True))
            t = p * dp
            ds = t - p * jnp.sum(t, axis=0, keepdims=True)
            return block, kb, vb, qh, dh, p.astype(BF16), ds

        def gradients(state, first_sample):
            block, kb, vb, qh, dh, pb, ds = state
            dsb = ds.astype(BF16)
            if first_sample:
                bsum_ref[...] = ds
            else:
                bsum_ref[...] += ds
            dk_refs[block][keys, :] += dot(dsb, qh)
            dv_refs[block][keys, :] += dot(pb, dh)
            att = own_head(dot_tn(pb, vb))
            dq_ref[block, qrows, :] = (own_head(dot_tn(dsb, kb)) * scale).astype(BF16)
            gate = g_ref[block, qrows, :]
            ga = gate * att
            gated_ref[block, qrows, :] = ga.astype(BF16)
            dgate_ref[block, qrows, :] = (gy_ref[block, qrows, :] * ga * (1.0 - gate)).astype(BF16)

        states = [products(s) for s in range(samples)]
        states = [softmax(state) for state in states]
        for s, state in enumerate(states):
            gradients(state, s == 0)
        total = bsum_ref[...]
        total_b = total.astype(BF16)
        pw_ref[...] += dot(pair_w, total_b)
        straight = total.T
        bsum_ref[...] = straight
        core = meta_ref[meta_ref.shape[0] - 1]
        width = heads * half_rows
        mine_ref[slot] = bsum_ref[pl.ds(pl.multiple_of(core * width, width), width), :]
        other_ref[slot] = bsum_ref[
            pl.ds(pl.multiple_of((1 - core) * width, width), width), :
        ].astype(BF16)
        return tok_sum + jnp.sum(jnp.where(same, total, 0.0), axis=0, keepdims=True)

    tok_sum = jnp.zeros((1, lanes), F32)
    first = 0
    for n, side in enumerate(sides):
        count = len(side.windows)
        tok_sum = lax.fori_loop(
            0, count, functools.partial(one_window, n, side, first), tok_sum
        )
        first += count

    if edge:
        ga_ref[...] = ga_in_ref[...]
    acc_kv = jnp.zeros((channels, 2 * channels), F32)
    acc_qg = jnp.zeros((channels, 2 * channels), F32)
    acc_o = jnp.zeros((channels, channels), F32)
    for n, side in enumerate(sides):
        queries = len(side.windows) * win_rows
        qrow = side.query_row
        for s in range(samples):
            block = n * samples + s
            for source, row, rows, at in side.pieces:
                dk = dk_refs[block][at : at + rows, :] * scale
                dv = dv_refs[block][at : at + rows, :]
                dkv_b = jnp.concatenate([dk.astype(BF16), dv.astype(BF16)], axis=1)
                part = dot_nt(dkv_b, w_kv)
                if source == "lo":
                    ga_lo_ref[s] = part.astype(BF16)
                elif source == "hi":
                    ga_hi_ref[s] = part.astype(BF16)
                elif edge:
                    ga_ref[s, row : row + rows, :] += part
                else:
                    ga_ref[s, row : row + rows, :] = part
                acc_kv = acc_kv + dot_tn(act_piece(source, row, rows, s), dkv_b)
            dqg = jnp.concatenate([dq_ref[block], dgate_ref[block]], axis=1)
            ga_ref[s, qrow : qrow + queries, :] += dot_nt(dqg, w_qg)
            acc_qg = acc_qg + dot_tn(act_ref[s, qrow : qrow + queries, :], dqg)
            acc_o = acc_o + dot_tn(gated_ref[block], gout_ref[s, qrow : qrow + queries, :])

    diag = lax.broadcasted_iota(jnp.int32, (win_rows * cp, lanes), 0) // cp == lane_row
    pw = jnp.where(diag, pw_ref[...], 0.0).reshape(win_rows, cp, lanes).sum(axis=0)
    parts = [
        acc_qg[:, :channels],
        acc_kv[:, :channels],
        acc_kv[:, channels:],
        acc_qg[:, channels:],
        acc_o,
    ]
    first_half, second_half = [], []
    left = out_half
    for part in parts:
        if left >= channels:
            first_half.append(part)
            left -= channels
        elif left > 0:
            first_half.append(part[:left])
            second_half.append(part[left:])
            left = 0
        else:
            second_half.append(part)
    tok_rows = jnp.where(
        lax.broadcasted_iota(jnp.int32, (SMALL_ROWS, lanes), 0) == 0, tok_sum, 0.0
    )
    at = 0
    for part in first_half + [pw] + second_half + [tok_rows]:
        rows = part.shape[0]
        if edge:
            acc_ref[at : at + rows, :] = part + acc_in_ref[at : at + rows, :]
        else:
            acc_ref[at : at + rows, :] = part
        at += rows


def pair_kernel(wpair_ref, m1_ref, r1_ref, m2_ref, r2_ref, out_ref, *, order, heads, cp):
    rows = m1_ref.shape[1]
    half_rows = rows // heads
    lane = lax.broadcasted_iota(jnp.int32, (1, rows), 1)
    pick = (
        lax.broadcasted_iota(jnp.int32, (heads, rows), 0)
        == lax.broadcasted_iota(jnp.int32, (heads, rows), 1) // half_rows
    ).astype(BF16)
    wlane = dot(wpair_ref[...], pick)
    wexp = jnp.concatenate(
        [jnp.where(lane % half_rows == i, wlane, 0.0) for i in range(half_rows)], axis=0
    ).astype(BF16)
    for which, (m_ref, r_ref) in enumerate(((m1_ref, r1_ref), (m2_ref, r2_ref))):
        for slot, window in enumerate(order[which]):
            total = (m_ref[slot] + r_ref[slot].astype(F32)).astype(BF16)
            out_ref[window] = dot(wexp, total).astype(BF16)


def per_device(
    act,
    grad_out,
    pair,
    w_query,
    w_key,
    w_value,
    w_gate,
    w_out,
    w_pair,
    w_token,
    offsets,
    atom_token,
    padding,
):
    samples, atoms, channels = act.shape
    windows = offsets.shape[0]
    win_rows = atoms // windows
    span = pair.shape[-1]
    cp, heads = w_pair.shape
    half_rows = win_rows // 2
    lanes = heads * win_rows
    ranges = lax.axis_size("atoms")
    cores = lax.axis_size("samples")
    assert cores == 2 and ranges & (ranges - 1) == 0
    core = lax.axis_index("samples")
    anchor = lax.axis_index("atoms") * atoms
    position = jnp.arange(atoms, dtype=jnp.int32)
    codes = jnp.where(position < atoms - padding[0], atom_token + 1, 0)
    starts = (
        jnp.clip(
            anchor + win_rows * jnp.arange(windows, dtype=jnp.int32) + offsets,
            0,
            ranges * atoms - span,
        )
        - anchor
    )
    edge_count = span // win_rows
    inner = tuple(range(edge_count, windows - edge_count))
    low, high = tuple(range(edge_count)), tuple(range(windows - edge_count, windows))
    own = edge_count * win_rows + span
    edge_rows = own + span
    index = jnp.arange(windows, dtype=jnp.int32)
    low_limit = jnp.where(
        index < edge_count, -span, jnp.where(index < windows - edge_count, 0, atoms - own)
    )
    high_limit = jnp.where(
        index < edge_count,
        own - span,
        jnp.where(index < windows - edge_count, atoms - span, atoms),
    )
    starts = jnp.clip(starts, low_limit, high_limit)
    meta = jnp.concatenate([starts, core[None].astype(jnp.int32)])
    qcode = jnp.broadcast_to(
        (atom_token + 1).astype(F32).reshape(windows, 2, 1, half_rows),
        (windows, 2, heads, half_rows),
    ).reshape(windows, lanes)
    codes_f = codes.astype(F32).reshape(1, atoms)

    def payload(first):
        part = lax.slice_in_dim(act, first, first + span, axis=1).reshape(-1, channels)
        code = lax.slice_in_dim(codes, first, first + span)[None]
        extra = jnp.concatenate(
            [code // CODE_BASE, code % CODE_BASE, jnp.zeros((CODE_ROWS - 2, span), jnp.int32)]
        )
        return jnp.concatenate([part, extra.astype(BF16)])

    up = [(i, i + 1) for i in range(ranges - 1)]
    down = [(j, i) for i, j in up]
    halo_lo = lax.ppermute(payload(atoms - span), "atoms", up)
    halo_hi = lax.ppermute(payload(0), "atoms", down)

    out_half = 5 * channels // 2
    acc_rows = 5 * channels + 2 * SMALL_ROWS
    geo = (samples, atoms, channels, heads, win_rows, span, cp, out_half)
    pair_flat = pair.reshape(windows, win_rows * cp, span)
    vmem = pl.BlockSpec(memory_space=pltpu.VMEM)
    smem = pl.BlockSpec(memory_space=pltpu.SMEM)
    hbm = pl.BlockSpec(memory_space=pl.ANY)
    width = heads * half_rows

    def call(sides, edge, args):
        count = sum(len(side.windows) for side in sides)
        queries = len(sides[0].windows) * win_rows
        rows = sides[0].rows
        blocks = len(sides) * samples
        out_shape = [jax.ShapeDtypeStruct((samples, atoms, channels), F32)]
        if edge:
            out_shape += [jax.ShapeDtypeStruct((samples, span, channels), BF16)] * 2
        out_shape += [
            jax.ShapeDtypeStruct((acc_rows, channels), F32),
            jax.ShapeDtypeStruct((count, width, span), F32),
            jax.ShapeDtypeStruct((count, width, span), BF16),
        ]
        per_query = (blocks, queries, channels)
        scratch = [
            pltpu.VMEM((count, win_rows * cp, span), BF16),
            pltpu.SemaphoreType.DMA((len(sides),)),
            pltpu.VMEM((win_rows * cp, lanes), BF16),
            pltpu.VMEM((win_rows * cp, lanes), F32),
            pltpu.VMEM((len(sides), rows, span), F32),
            pltpu.VMEM(per_query, BF16),
            pltpu.VMEM(per_query, BF16),
            pltpu.VMEM(per_query, F32),
            pltpu.VMEM(per_query, F32),
            pltpu.VMEM(per_query, BF16),
            pltpu.VMEM(per_query, BF16),
            pltpu.VMEM(per_query, BF16),
            pltpu.VMEM((span, lanes), F32),
            pltpu.VMEM((span, lanes), F32),
        ]
        scratch += [pltpu.VMEM((rows, channels), F32)] * (4 * blocks)
        units = 6 * count * samples + 8 * count + 14 * blocks
        return pl.pallas_call(
            functools.partial(attention_kernel, geo, sides, edge),
            out_shape=out_shape,
            in_specs=[smem] * 2 + [vmem] * 4 + [hbm] + [vmem] * (len(args) - 7),
            out_specs=[vmem] * len(out_shape),
            scratch_shapes=scratch,
            compiler_params=pltpu.CompilerParams(vmem_limit_bytes=VMEM_LIMIT),
            cost_estimate=pl.CostEstimate(
                flops=2 * units * 128 * 128 * 128 * 4,
                bytes_accessed=12_000_000,
                transcendentals=count * samples * span * lanes,
            ),
        )(*args)

    common = (
        meta,
        w_token,
        act,
        grad_out,
        codes_f,
        qcode,
        pair_flat,
        w_query,
        w_key,
        w_value,
        w_gate,
        w_out,
        w_pair,
    )
    inner_side = Side(inner, span, atoms, [("act", 0, atoms, 0)], 0)
    ga1, acc1, mine1, other1 = call([inner_side], False, common)
    swap = [(0, 1), (1, 0)]
    recv1 = lax.ppermute(other1, "samples", swap)

    low_side = Side(low, 0, edge_rows, [("lo", 0, span, 0), ("act", 0, own, span)], -span)
    high_side = Side(
        high,
        atoms - span,
        edge_rows,
        [("act", atoms - own, own, 0), ("hi", 0, span, own)],
        atoms - own,
    )
    ga2, ga_lo, ga_hi, acc, mine2, other2 = call(
        [low_side, high_side], True, common + (halo_lo, halo_hi, ga1, acc1)
    )
    recv2 = lax.ppermute(other2, "samples", swap)
    from_upper = lax.ppermute(ga_lo, "atoms", down)
    from_lower = lax.ppermute(ga_hi, "atoms", up)

    part_rows = acc_rows // 2
    wide = part_rows - SMALL_ROWS

    def encode(value):
        small = value[wide:]
        top = lax.reduce_precision(value, 8, 7)
        return jnp.concatenate([top, small - top[wide:]]).astype(BF16)

    def decode(sent):
        sent = sent.astype(F32)
        return jnp.concatenate(
            [sent[:wide], sent[wide : wide + SMALL_ROWS] + sent[wide + SMALL_ROWS :]]
        )

    acc = acc.reshape(2, part_rows, channels)
    mine = encode(lax.dynamic_index_in_dim(acc, core, 0, keepdims=False))
    other = encode(lax.dynamic_index_in_dim(acc, 1 - core, 0, keepdims=False))
    total = decode(mine) + decode(lax.ppermute(other, "samples", swap))
    step = 1
    while step < ranges:
        sent = encode(total)
        got = lax.ppermute(sent, "atoms", [(i, i ^ step) for i in range(ranges)])
        total = decode(sent) + decode(got)
        step *= 2
    sent = encode(total)
    got = lax.ppermute(sent, "samples", swap)
    is_first = core == 0
    first = decode(jnp.where(is_first, sent, got))
    second = decode(jnp.where(is_first, got, sent))
    grad_weights = jnp.concatenate([first[:wide], second[:wide]]).reshape(5, channels, channels)
    grad_pair_weight = first[wide:].reshape(cp, 2, heads, half_rows).sum(axis=(1, 3))
    grad_token_weight = second[wide].reshape(2, heads, half_rows).sum(axis=(0, 2))

    grad_pair = pl.pallas_call(
        functools.partial(pair_kernel, order=(inner, low + high), heads=heads, cp=cp),
        out_shape=jax.ShapeDtypeStruct((windows, half_rows * cp, span), BF16),
        in_specs=[vmem] * 5,
        out_specs=vmem,
        compiler_params=pltpu.CompilerParams(vmem_limit_bytes=VMEM_LIMIT),
        cost_estimate=pl.CostEstimate(
            flops=2 * windows * 256 * 256 * 256, bytes_accessed=4_000_000, transcendentals=0
        ),
    )(w_pair, mine1, recv1, mine2, recv2).reshape(windows, half_rows, cp, span)

    grad_act = (
        ga2.at[:, :span]
        .add(from_lower.astype(F32))
        .at[:, atoms - span :]
        .add(from_upper.astype(F32))
        .astype(BF16)
    )
    return (grad_act, grad_pair, grad_weights, grad_pair_weight, grad_token_weight)


def solution(mesh):
    in_specs = (
        P("samples", ("groups", "atoms"), None),
        P("samples", ("groups", "atoms"), None),
        P(("groups", "atoms"), None, None, None),
        P(),
        P(),
        P(),
        P(),
        P(),
        P(),
        P(),
        P(("groups", "atoms")),
        P(("groups", "atoms")),
        P(("groups", "atoms")),
    )
    out_specs = (
        P("samples", ("groups", "atoms"), None),
        P(("groups", "atoms"), "samples", None, None),
        P("groups", None, None),
        P("groups", None),
        P("groups"),
    )
    return jax.shard_map(
        per_device, mesh=mesh, in_specs=in_specs, out_specs=out_specs, check_vma=False
    )
```

```python
import functools
import math

import jax
import jax.numpy as jnp
from jax import lax
from jax.experimental import pallas as pl
from jax.experimental.pallas import tpu as pltpu
from jax.sharding import PartitionSpec as P

BF16 = jnp.bfloat16
F32 = jnp.float32
MASKED = -1000000000.0
LOG2E = math.log2(math.e)
CODE_ROWS = 16
CODE_BASE = 128
SMALL_ROWS = 16
VMEM_LIMIT = 56 * 1024 * 1024
EARLY_SHARE = 5


def dot(a, b):
    return lax.dot_general(a, b, (((1,), (0,)), ((), ())), preferred_element_type=F32)


def dot_nt(a, b):
    return lax.dot_general(a, b, (((1,), (1,)), ((), ())), preferred_element_type=F32)


def dot_tn(a, b):
    return lax.dot_general(a, b, (((0,), (0,)), ((), ())), preferred_element_type=F32)


def column_of(row, span):
    return jnp.broadcast_to(row, (span, row.shape[-1])).T


class Side:
    def __init__(self, windows, win_rows, rows, pieces, origin):
        self.first = windows[0]
        self.count = len(windows)
        self.queries = len(windows) * win_rows
        self.query_row = windows[0] * win_rows
        self.rows = rows
        self.pieces = pieces
        self.origin = origin


def payload_kernel(high_ref, low_ref, tok_ref, padding_ref, up_ref, down_ref):
    samples, span, _ = high_ref.shape
    rows = tok_ref.shape[0]
    atoms = rows * span
    index = lax.broadcasted_iota(jnp.int32, (CODE_ROWS, span), 0)
    place = lax.broadcasted_iota(jnp.int32, (1, span), 1)
    for out_ref, act_ref, row in ((up_ref, high_ref, rows - 1), (down_ref, low_ref, 0)):
        for s in range(samples):
            out_ref[s * span : (s + 1) * span, :] = act_ref[s]
        live = place + row * span < atoms - padding_ref[0]
        code = jnp.where(live, tok_ref[row : row + 1, :] + 1, 0)
        top, low = code // CODE_BASE, code % CODE_BASE
        both = jnp.where(index == 0, top, jnp.where(index == 1, low, 0))
        out_ref[samples * span :, :] = both.astype(F32).astype(BF16)


def attention_kernel(geo, sides, edge, chained, last, *refs):
    samples, atoms, channels, heads, win_rows, span, cp, out_half = geo
    refs = list(refs)
    take = lambda n: [refs.pop(0) for _ in range(n)]
    place_ref, offsets_ref, padding_ref, wtok_ref = take(4)
    tok_ref, act_hbm, gout_hbm, pair_hbm = take(4)
    wq_ref, wk_ref, wv_ref, wg_ref, wo_ref, wpair_ref = take(6)
    halo = {}
    if edge:
        halo["lo"], halo["hi"] = take(2)
    if chained:
        (acc_in_ref,) = take(1)
    ga_refs = take(len(sides))
    if edge:
        ga_lo_ref, ga_hi_ref = take(2)
    if last:
        acc_mine_ref, acc_other_ref = take(2)
    else:
        (acc_ref,) = take(1)
    mine_ref, other_ref = take(2)
    pair_ref, pair_sem, wexp_ref, pw_ref, code_ref, qcode_ref, halo_code_ref = take(7)
    act_ref, gout_ref, in_sem, q_ref, datt_ref, g_ref, gy_ref = take(7)
    dq_ref, dgate_ref, gated_ref, bias_ref, bsum_ref = take(5)
    if last:
        (acc_ref,) = take(1)
    n_blocks = len(sides) * samples
    k_refs = take(n_blocks)
    v_refs = take(n_blocks)
    dk_refs = take(n_blocks)
    dv_refs = take(n_blocks)

    half_rows = win_rows // 2
    head_dim = channels // heads
    scale = 1.0 / math.sqrt(head_dim)
    anchor = place_ref[0] * atoms
    all_atoms = place_ref[2] * atoms
    core = place_ref[1]

    block_copies = []
    for n, side in enumerate(sides):
        for s in range(samples):
            block = n * samples + s
            mine = []
            for source, row, rows, at in side.pieces:
                if source == "act":
                    origin = act_hbm.at[s, pl.ds(row, rows)]
                else:
                    origin = halo[source].at[pl.ds(s * span, rows)]
                mine.append((origin, act_ref.at[block, pl.ds(at, rows)]))
            mine.append(
                (gout_hbm.at[s, pl.ds(side.query_row, side.queries)], gout_ref.at[block])
            )
            block_copies.append(
                [
                    pltpu.make_async_copy(source, target, in_sem.at[block, i])
                    for i, (source, target) in enumerate(mine)
                ]
            )
    code_copies = []
    if edge:
        for i, name in enumerate(("lo", "hi")):
            code_copies.append(
                pltpu.make_async_copy(
                    halo[name].at[pl.ds(samples * span, CODE_ROWS)],
                    halo_code_ref.at[i],
                    pair_sem.at[len(sides) + i],
                )
            )
    pair_copies = []
    first = 0
    for n, side in enumerate(sides):
        pair_copies.append(
            pltpu.make_async_copy(
                pair_hbm.at[pl.ds(side.first, side.count)],
                pair_ref.at[pl.ds(first, side.count)],
                pair_sem.at[n],
            )
        )
        first += side.count
    for copy in code_copies:
        copy.start()
    for copies in block_copies:
        for copy in copies:
            copy.start()
    for copy in pair_copies:
        copy.start()

    lane = lax.broadcasted_iota(jnp.int32, (1, channels), 1)
    head_masks = [(lane // head_dim == h).astype(F32) for h in range(heads)]
    head_masks_b = [m.astype(BF16) for m in head_masks]

    lanes = 2 * heads * half_rows
    s_lane = lax.broadcasted_iota(jnp.int32, (1, lanes), 1)
    lane_head = (s_lane // half_rows) % heads
    lane_row = (s_lane // (heads * half_rows)) * half_rows + s_lane % half_rows
    wtok = jnp.zeros((1, lanes), F32)
    for h in range(heads):
        wtok = jnp.where(lane_head == h, wtok_ref[h], wtok)
    pick = (
        lax.broadcasted_iota(jnp.int32, (heads, lanes), 0)
        == (lax.broadcasted_iota(jnp.int32, (heads, lanes), 1) // half_rows) % heads
    ).astype(BF16)
    wlane = dot_tn(wpair_ref[...], pick).astype(BF16)
    for i in range(win_rows):
        wexp_ref[i * cp : (i + 1) * cp, :] = jnp.where(lane_row == i, wlane, 0.0).astype(BF16)
    pw_ref[...] = jnp.zeros_like(pw_ref)

    per_row = span // win_rows
    code = tok_ref[...] + 1
    top = (code // CODE_BASE).astype(F32).astype(BF16)
    low = (code % CODE_BASE).astype(F32).astype(BF16)
    source_lane = lax.broadcasted_iota(jnp.int32, (span, lanes), 0)
    for m in range(per_row):
        spread = (source_lane == m * win_rows + lane_row).astype(F32).astype(BF16)
        qcode_ref[m, : code.shape[0], :] = dot(top, spread) * CODE_BASE + dot(low, spread)

    live = jnp.where(
        lax.broadcasted_iota(jnp.int32, code.shape, 0) * span
        + lax.broadcasted_iota(jnp.int32, code.shape, 1)
        < atoms - padding_ref[0],
        code,
        0,
    ).astype(F32)
    for r in range(code.shape[0]):
        if any(
            r * span < row + rows and row < (r + 1) * span
            for side in sides
            for source, row, rows, _ in side.pieces
            if source == "act"
        ):
            code_ref[(r + 1) * span : (r + 2) * span, :] = column_of(live[r : r + 1], span)
    for copy in code_copies:
        copy.wait()
    if edge:
        for i, at in enumerate((0, atoms + span)):
            two = halo_code_ref[i].astype(F32)
            row = two[0:1, :] * CODE_BASE + two[1:2, :]
            code_ref[at : at + span, :] = column_of(row, span)

    w_kv = jnp.concatenate([wk_ref[...], wv_ref[...]], axis=1)
    w_qg = jnp.concatenate([wq_ref[...], wg_ref[...]], axis=1)
    for n, side in enumerate(sides):
        for s in range(samples):
            block = n * samples + s
            for copy in block_copies[block]:
                copy.wait()
            kv = dot(act_ref[block], w_kv)
            k_refs[block][...] = kv[:, :channels]
            v_refs[block][...] = kv[:, channels:]
            dk_refs[block][...] = jnp.zeros_like(dk_refs[block])
            dv_refs[block][...] = jnp.zeros_like(dv_refs[block])
            at = side.query_row - side.origin
            qg = dot(act_ref[block, at : at + side.queries, :], w_qg)
            q_ref[block] = qg[:, :channels].astype(BF16)
            gate = jax.nn.sigmoid(qg[:, channels:])
            gy = dot_nt(gout_ref[block], wo_ref[...])
            g_ref[block] = gate
            gy_ref[block] = gy
            datt_ref[block] = (gy * gate).astype(BF16)

    for copy in pair_copies:
        copy.wait()

    def by_head(rows):
        return jnp.concatenate(
            [
                rows[half * half_rows : (half + 1) * half_rows] * head_masks_b[h]
                for half in range(2)
                for h in range(heads)
            ],
            axis=0,
        )

    def own_head(wide):
        halves = []
        for half in range(2):
            total = None
            for h in range(heads):
                at = (half * heads + h) * half_rows
                term = wide[at : at + half_rows] * head_masks[h]
                total = term if total is None else total + term
            halves.append(total)
        return jnp.concatenate(halves, axis=0)

    def one_window(n, side, first, w, tok_sum):
        slot = first + w
        window = side.first + w
        start = jnp.clip(
            anchor + window * win_rows + offsets_ref[window], 0, all_atoms - span
        ) - (anchor + side.origin)
        start = jnp.clip(start, 0, side.rows - span)
        key_codes = code_ref[pl.ds(start + (side.origin + span), span), :]
        query_codes = qcode_ref[window % per_row, pl.ds(window // per_row, 1), :]
        same = key_codes == query_codes
        pair_w = pair_ref[slot]
        bias = dot_tn(pair_w, wexp_ref[...]) + jnp.where(same, wtok, 0.0)
        bias_ref[...] = jnp.where(key_codes > 0.0, bias, MASKED) * LOG2E
        qrows = pl.ds(pl.multiple_of(w * win_rows, win_rows), win_rows)
        keys = pl.ds(start, span)

        def products(s):
            block = n * samples + s
            kb = k_refs[block][keys, :].astype(BF16)
            vb = v_refs[block][keys, :].astype(BF16)
            qh = by_head(q_ref[block, qrows, :])
            dh = by_head(datt_ref[block, qrows, :])
            return block, kb, vb, qh, dh, dot_nt(kb, qh), dot_nt(vb, dh)

        def softmax(state):
            block, kb, vb, qh, dh, x, dp = state
            x = x * (scale * LOG2E) + bias_ref[...]
            e = jnp.exp2(x - jnp.max(x, axis=0, keepdims=True))
            p = e * (1.0 / jnp.sum(e, axis=0, keepdims=True))
            t = p * dp
            ds = t - p * jnp.sum(t, axis=0, keepdims=True)
            return block, kb, vb, qh, dh, p.astype(BF16), ds

        def gradients(state, first_sample):
            block, kb, vb, qh, dh, pb, ds = state
            dsb = ds.astype(BF16)
            if first_sample:
                bsum_ref[...] = ds
            else:
                bsum_ref[...] += ds
            dk_refs[block][keys, :] += dot(dsb, qh)
            dv_refs[block][keys, :] += dot(pb, dh)
            att = own_head(dot_tn(pb, vb))
            dq_ref[block, qrows, :] = (own_head(dot_tn(dsb, kb)) * scale).astype(BF16)
            gate = g_ref[block, qrows, :]
            ga = gate * att
            gated_ref[block, qrows, :] = ga.astype(BF16)
            dgate_ref[block, qrows, :] = (gy_ref[block, qrows, :] * ga * (1.0 - gate)).astype(BF16)

        states = [products(s) for s in range(samples)]
        states = [softmax(state) for state in states]
        for s, state in enumerate(states):
            gradients(state, s == 0)
        total = bsum_ref[...]
        total_b = total.astype(BF16)
        pw_ref[...] += dot(pair_w, total_b)
        straight = total.T
        bsum_ref[...] = straight
        width = heads * half_rows
        mine_ref[slot] = bsum_ref[pl.ds(pl.multiple_of(core * width, width), width), :]
        other_ref[slot] = bsum_ref[
            pl.ds(pl.multiple_of((1 - core) * width, width), width), :
        ].astype(BF16)
        return tok_sum + jnp.sum(jnp.where(same, total, 0.0), axis=0, keepdims=True)

    tok_sum = jnp.zeros((1, lanes), F32)
    first = 0
    for n, side in enumerate(sides):
        tok_sum = lax.fori_loop(
            0, side.count, functools.partial(one_window, n, side, first), tok_sum
        )
        first += side.count

    acc_kv = jnp.zeros((channels, 2 * channels), F32)
    acc_qg = jnp.zeros((channels, 2 * channels), F32)
    acc_o = jnp.zeros((channels, channels), F32)
    for n, side in enumerate(sides):
        at = side.query_row - side.origin
        for s in range(samples):
            block = n * samples + s
            dkv_b = jnp.concatenate(
                [(dk_refs[block][...] * scale).astype(BF16), dv_refs[block][...].astype(BF16)],
                axis=1,
            )
            dqg = jnp.concatenate([dq_ref[block], dgate_ref[block]], axis=1)
            part = dot_nt(dkv_b, w_kv)
            middle = part[at : at + side.queries] + dot_nt(dqg, w_qg)
            runs = [(0, part[:at]), (at, middle), (at + side.queries, part[at + side.queries :])]
            for run_at, run in runs:
                if run.shape[0] == 0:
                    continue
                run = run.astype(BF16)
                for source, _, rows, piece_at in side.pieces:
                    low = max(run_at, piece_at)
                    high = min(run_at + run.shape[0], piece_at + rows)
                    if low >= high:
                        continue
                    value = run[low - run_at : high - run_at]
                    if source == "lo":
                        ga_lo_ref[s, low - piece_at : high - piece_at, :] = value
                    elif source == "hi":
                        ga_hi_ref[s, low - piece_at : high - piece_at, :] = value
                    else:
                        ga_refs[n][s, low - piece_at : high - piece_at, :] = value
            acc_kv = acc_kv + dot_tn(act_ref[block], dkv_b)
            acc_qg = acc_qg + dot_tn(act_ref[block, at : at + side.queries, :], dqg)
            acc_o = acc_o + dot_tn(gated_ref[block], gout_ref[block])

    diag = lax.broadcasted_iota(jnp.int32, (win_rows * cp, lanes), 0) // cp == lane_row
    pw = jnp.where(diag, pw_ref[...], 0.0).reshape(win_rows, cp, lanes).sum(axis=0)
    parts = [
        acc_qg[:, :channels],
        acc_kv[:, :channels],
        acc_kv[:, channels:],
        acc_qg[:, channels:],
        acc_o,
    ]
    first_half, second_half = [], []
    left = out_half
    for part in parts:
        if left >= channels:
            first_half.append(part)
            left -= channels
        elif left > 0:
            first_half.append(part[:left])
            second_half.append(part[left:])
            left = 0
        else:
            second_half.append(part)
    tok_rows = jnp.where(
        lax.broadcasted_iota(jnp.int32, (SMALL_ROWS, lanes), 0) == 0, tok_sum, 0.0
    )
    for half, group in enumerate((first_half + [pw], second_half + [tok_rows])):
        at = 0
        for part in group:
            rows = part.shape[0]
            if chained:
                part = part + acc_in_ref[half, at : at + rows, :]
            acc_ref[half, at : at + rows, :] = part
            at += rows
    if last:
        acc_mine_ref[...] = acc_ref[core]
        value = acc_ref[1 - core]
        wide = value.shape[0] - SMALL_ROWS
        top = value.astype(BF16)
        acc_other_ref[: wide + SMALL_ROWS, :] = top
        rest = value[wide:] - top[wide:].astype(F32)
        acc_other_ref[wide + SMALL_ROWS :, :] = rest.astype(BF16)


def pair_kernel(wpair_ref, *refs, order, heads, cp):
    out_ref = refs[-1]
    rows = refs[0].shape[1]
    half_rows = rows // heads
    lane = lax.broadcasted_iota(jnp.int32, (1, rows), 1)
    pick = (
        lax.broadcasted_iota(jnp.int32, (heads, rows), 0)
        == lax.broadcasted_iota(jnp.int32, (heads, rows), 1) // half_rows
    ).astype(BF16)
    wlane = dot_tn(wpair_ref[...], pick)
    wexp = jnp.concatenate(
        [jnp.where(lane % half_rows == i, wlane, 0.0) for i in range(half_rows)], axis=0
    ).astype(BF16)
    for which, group in enumerate(order):
        m_ref, r_ref = refs[2 * which], refs[2 * which + 1]
        for slot, window in enumerate(group):
            total = (m_ref[slot] + r_ref[slot].astype(F32)).astype(BF16)
            out_ref[window] = dot(wexp, total).astype(BF16)


def act_sum_kernel(firsts, *refs):
    out_ref = refs[-1]
    atoms = out_ref.shape[1]
    marks = {0, atoms}
    for first, ref in zip(firsts, refs):
        marks |= {first, first + ref.shape[1]}
    marks = sorted(marks)
    for low, high in zip(marks[:-1], marks[1:]):
        total = None
        for first, ref in zip(firsts, refs):
            if first <= low and high <= first + ref.shape[1]:
                term = ref[:, low - first : high - first, :].astype(F32)
                total = term if total is None else total + term
        out_ref[:, low:high, :] = total.astype(BF16)


def finish_kernel(place_ref, sent_ref, got_ref, gw_ref, gpw_ref, gtok_ref, *, heads):
    rows = sent_ref.shape[0]
    wide = rows - 2 * SMALL_ROWS
    channels = gw_ref.shape[1]
    is_first = place_ref[1] == 0
    sent, got = sent_ref[...].astype(F32), got_ref[...].astype(F32)
    first = jnp.where(is_first, sent, got)
    second = jnp.where(is_first, got, sent)
    gw_ref[:wide, :] = first[:wide]
    gw_ref[wide:, :] = second[:wide]
    pw = first[wide : wide + SMALL_ROWS] + first[wide + SMALL_ROWS :]
    tok = second[wide : wide + 1] + second[wide + SMALL_ROWS : wide + SMALL_ROWS + 1]
    half_rows = channels // (2 * heads)
    head = (lax.broadcasted_iota(jnp.int32, (heads, channels), 1) // half_rows) % heads
    pick = (head == lax.broadcasted_iota(jnp.int32, (heads, channels), 0)).astype(F32)
    gpw_ref[...] = lax.dot_general(
        pick,
        pw,
        (((1,), (1,)), ((), ())),
        precision=lax.Precision.HIGHEST,
        preferred_element_type=F32,
    )
    for h in range(heads):
        gtok_ref[h] = jnp.sum(tok * pick[h : h + 1])


def per_device(
    act,
    grad_out,
    pair,
    w_query,
    w_key,
    w_value,
    w_gate,
    w_out,
    w_pair,
    w_token,
    offsets,
    atom_token,
    padding,
):
    samples, atoms, channels = act.shape
    windows = offsets.shape[0]
    win_rows = atoms // windows
    span = pair.shape[-1]
    cp, heads = w_pair.shape
    half_rows = win_rows // 2
    lanes = heads * win_rows
    ranges = lax.axis_size("atoms")
    cores = lax.axis_size("samples")
    assert cores == 2 and ranges & (ranges - 1) == 0
    core = lax.axis_index("samples")
    place = jnp.stack([lax.axis_index("atoms"), core, jnp.int32(ranges)]).astype(jnp.int32)
    tok = atom_token.reshape(atoms // span, span)
    w_pair_t = w_pair.T
    vmem = pl.BlockSpec(memory_space=pltpu.VMEM)
    smem = pl.BlockSpec(memory_space=pltpu.SMEM)
    hbm = pl.BlockSpec(memory_space=pl.ANY)

    up = [(i, i + 1) for i in range(ranges - 1)]
    down = [(j, i) for i, j in up]
    last_block = atoms // span - 1
    to_up, to_down = pl.pallas_call(
        payload_kernel,
        out_shape=[jax.ShapeDtypeStruct((samples * span + CODE_ROWS, channels), BF16)] * 2,
        grid=(1,),
        in_specs=[
            pl.BlockSpec((samples, span, channels), lambda i: (0, last_block, 0)),
            pl.BlockSpec((samples, span, channels), lambda i: (0, 0, 0)),
            vmem,
            smem,
        ],
        out_specs=[vmem, vmem],
    )(act, act, tok, padding)
    halo_lo = lax.ppermute(to_up, "atoms", up)
    halo_hi = lax.ppermute(to_down, "atoms", down)

    out_half = 5 * channels // 2
    part_rows = out_half + SMALL_ROWS
    coded_rows = part_rows + SMALL_ROWS
    geo = (samples, atoms, channels, heads, win_rows, span, cp, out_half)
    pair_flat = pair.reshape(windows, win_rows * cp, span)
    width = heads * half_rows
    common = (
        place,
        offsets,
        padding,
        w_token,
        tok,
        act,
        grad_out,
        pair_flat,
        w_query,
        w_key,
        w_value,
        w_gate,
        w_out,
        w_pair_t,
    )
    shape = jax.ShapeDtypeStruct

    def call(sides, halos=(), acc_in=None, last=False):
        edge, chained = len(halos) > 0, acc_in is not None
        args = common + tuple(halos) + ((acc_in,) if chained else ())
        in_specs = [smem] * 4 + [vmem] + [hbm] * 3 + [vmem] * 6 + [hbm] * len(halos)
        in_specs += [vmem] * chained
        count = sum(side.count for side in sides)
        queries, rows = sides[0].queries, sides[0].rows
        blocks = len(sides) * samples
        own_rows = [sum(p[2] for p in side.pieces if p[0] == "act") for side in sides]
        out_shape = [shape((samples, n, channels), BF16) for n in own_rows]
        if edge:
            out_shape += [shape((samples, span, channels), BF16)] * 2
        if last:
            out_shape += [shape((part_rows, channels), F32), shape((coded_rows, channels), BF16)]
        else:
            out_shape += [shape((2, part_rows, channels), F32)]
        out_shape += [shape((count, width, span), F32), shape((count, width, span), BF16)]
        per_query = (blocks, queries, channels)
        scratch = [
            pltpu.VMEM((count, win_rows * cp, span), BF16),
            pltpu.SemaphoreType.DMA((len(sides) + 2,)),
            pltpu.VMEM((win_rows * cp, lanes), BF16),
            pltpu.VMEM((win_rows * cp, lanes), F32),
            pltpu.VMEM((atoms + 2 * span, span), F32),
            pltpu.VMEM((span // win_rows, -(-atoms // span // 8) * 8, lanes), F32),
            pltpu.VMEM((2, CODE_ROWS, span), BF16),
            pltpu.VMEM((blocks, rows, channels), BF16),
            pltpu.VMEM(per_query, BF16),
            pltpu.SemaphoreType.DMA((blocks, 3)),
            pltpu.VMEM(per_query, BF16),
            pltpu.VMEM(per_query, BF16),
            pltpu.VMEM(per_query, F32),
            pltpu.VMEM(per_query, F32),
            pltpu.VMEM(per_query, BF16),
            pltpu.VMEM(per_query, BF16),
            pltpu.VMEM(per_query, BF16),
            pltpu.VMEM((span, lanes), F32),
            pltpu.VMEM((span, lanes), F32),
        ]
        if last:
            scratch += [pltpu.VMEM((2, part_rows, channels), F32)]
        scratch += [pltpu.VMEM((rows, channels), F32)] * (4 * blocks)
        units = 6 * count * samples + 8 * count + 14 * blocks
        return pl.pallas_call(
            functools.partial(attention_kernel, geo, sides, edge, chained, last),
            out_shape=out_shape,
            in_specs=in_specs,
            out_specs=[vmem] * len(out_shape),
            scratch_shapes=scratch,
            compiler_params=pltpu.CompilerParams(vmem_limit_bytes=VMEM_LIMIT),
            cost_estimate=pl.CostEstimate(
                flops=2 * units * 128 * 128 * 128 * 4,
                bytes_accessed=12_000_000,
                transcendentals=count * samples * span * lanes,
            ),
        )(*args)

    edge_count = span // win_rows
    early_count = (windows - 2 * edge_count) * EARLY_SHARE // 12
    early = tuple(range(edge_count, edge_count + early_count))
    late = tuple(range(edge_count + early_count, windows - edge_count))
    low, high = tuple(range(edge_count)), tuple(range(windows - edge_count, windows))
    early_end = (early[-1] + 1) * win_rows + span
    late_first = late[0] * win_rows - span
    own = edge_count * win_rows + span
    swap = [(0, 1), (1, 0)]

    early_side = Side(early, win_rows, early_end, [("act", 0, early_end, 0)], 0)
    ga_early, acc, mine1, other1 = call([early_side])
    recv1 = lax.ppermute(other1, "samples", swap)

    low_side = Side(low, win_rows, own + span, [("lo", 0, span, 0), ("act", 0, own, span)], -span)
    high_side = Side(
        high,
        win_rows,
        own + span,
        [("act", atoms - own, own, 0), ("hi", 0, span, own)],
        atoms - own,
    )
    ga_low, ga_high, ga_lo, ga_hi, acc, mine2, other2 = call(
        [low_side, high_side], (halo_lo, halo_hi), acc
    )
    recv2 = lax.ppermute(other2, "samples", swap)
    from_upper = lax.ppermute(ga_lo, "atoms", down)
    from_lower = lax.ppermute(ga_hi, "atoms", up)

    late_rows = atoms - late_first
    late_side = Side(
        late, win_rows, late_rows, [("act", late_first, late_rows, 0)], late_first
    )
    ga_late, acc_mine, acc_other, mine3, other3 = call([late_side], (), acc, True)

    wide = out_half

    def encode(value):
        top = lax.reduce_precision(value, 8, 7)
        return jnp.concatenate([top, value[wide:] - top[wide:]]).astype(BF16)

    def decode(sent):
        sent = sent.astype(F32)
        return jnp.concatenate(
            [sent[:wide], sent[wide : wide + SMALL_ROWS] + sent[wide + SMALL_ROWS :]]
        )

    acc_other, other3, from_upper, from_lower = lax.optimization_barrier(
        (acc_other, other3, from_upper, from_lower)
    )
    recv3 = lax.ppermute(other3, "samples", swap)
    total = acc_mine + decode(lax.ppermute(acc_other, "samples", swap))
    grad_pair = pl.pallas_call(
        functools.partial(pair_kernel, order=(early, low + high, late), heads=heads, cp=cp),
        out_shape=shape((windows, half_rows * cp, span), BF16),
        in_specs=[vmem] * 7,
        out_specs=vmem,
        compiler_params=pltpu.CompilerParams(vmem_limit_bytes=VMEM_LIMIT),
        cost_estimate=pl.CostEstimate(
            flops=2 * windows * 256 * 256 * 256, bytes_accessed=4_000_000, transcendentals=0
        ),
    )(w_pair_t, mine1, recv1, mine2, recv2, mine3, recv3)

    pieces = [
        (0, ga_early),
        (late_first, ga_late),
        (0, ga_low),
        (atoms - own, ga_high),
        (0, from_lower),
        (atoms - span, from_upper),
    ]
    grad_act = pl.pallas_call(
        functools.partial(act_sum_kernel, [first for first, _ in pieces]),
        out_shape=shape((samples, atoms, channels), BF16),
        grid=(2,),
        in_specs=[
            pl.BlockSpec((samples // 2,) + part.shape[1:], lambda s: (s, 0, 0))
            for _, part in pieces
        ],
        out_specs=pl.BlockSpec((samples // 2, atoms, channels), lambda s: (s, 0, 0)),
        compiler_params=pltpu.CompilerParams(vmem_limit_bytes=VMEM_LIMIT),
        cost_estimate=pl.CostEstimate(
            flops=4 * samples * atoms * channels, bytes_accessed=6_000_000, transcendentals=0
        ),
    )(*[part for _, part in pieces])
    step = ranges // 2
    while step >= 1:
        if step == ranges // 4:
            total, grad_pair = lax.optimization_barrier((total, grad_pair))
        if step == ranges // 8:
            total, grad_act = lax.optimization_barrier((total, grad_act))
        sent = encode(total)
        got = lax.ppermute(sent, "atoms", [(i, i ^ step) for i in range(ranges)])
        total = decode(sent) + decode(got)
        step //= 2
    sent = encode(total)
    got = lax.ppermute(sent, "samples", swap)
    grad_weights, grad_pair_weight, grad_token_weight = pl.pallas_call(
        functools.partial(finish_kernel, heads=heads),
        out_shape=[
            shape((5 * channels, channels), F32),
            shape((heads, cp), F32),
            shape((heads,), F32),
        ],
        in_specs=[smem, vmem, vmem],
        out_specs=[vmem, vmem, smem],
    )(place, sent, got)

    return (
        grad_act,
        grad_pair.reshape(windows, half_rows, cp, span),
        grad_weights.reshape(5, channels, channels),
        grad_pair_weight.T,
        grad_token_weight,
    )


def solution(mesh):
    in_specs = (
        P("samples", ("groups", "atoms"), None),
        P("samples", ("groups", "atoms"), None),
        P(("groups", "atoms"), None, None, None),
        P(),
        P(),
        P(),
        P(),
        P(),
        P(),
        P(),
        P(("groups", "atoms")),
        P(("groups", "atoms")),
        P(("groups", "atoms")),
    )
    out_specs = (
        P("samples", ("groups", "atoms"), None),
        P(("groups", "atoms"), "samples", None, None),
        P("groups", None, None),
        P("groups", None),
        P("groups"),
    )
    return jax.shard_map(
        per_device, mesh=mesh, in_specs=in_specs, out_specs=out_specs, check_vma=False
    )
```

```python
import functools
import math

import jax
import jax.numpy as jnp
from jax import lax
from jax.experimental import pallas as pl
from jax.experimental.pallas import tpu as pltpu
from jax.sharding import PartitionSpec as P

BF16 = jnp.bfloat16
F32 = jnp.float32
MASKED = -1000000000.0
LOG2E = math.log2(math.e)
CODE_ROWS = 16
CODE_BASE = 128
SMALL_ROWS = 16
VMEM_LIMIT = 56 * 1024 * 1024
EARLY_SHARE = 6


def dot(a, b):
    return lax.dot_general(a, b, (((1,), (0,)), ((), ())), preferred_element_type=F32)


def dot_nt(a, b):
    return lax.dot_general(a, b, (((1,), (1,)), ((), ())), preferred_element_type=F32)


def dot_tn(a, b):
    return lax.dot_general(a, b, (((0,), (0,)), ((), ())), preferred_element_type=F32)


def column_of(row, span):
    return jnp.broadcast_to(row, (span, row.shape[-1])).T


class Side:
    def __init__(self, windows, win_rows, rows, pieces, origin):
        self.first = windows[0]
        self.count = len(windows)
        self.queries = len(windows) * win_rows
        self.query_row = windows[0] * win_rows
        self.rows = rows
        self.pieces = pieces
        self.origin = origin


class HaloCopy:
    def __init__(self, is_odd, when_odd, when_even, target, sem):
        self.is_odd = is_odd
        self.options = [pltpu.make_async_copy(s, target, sem) for s in (when_even, when_odd)]

    def start(self):
        pl.when(self.is_odd)(self.options[1].start)
        pl.when(jnp.logical_not(self.is_odd))(self.options[0].start)

    def wait(self):
        self.options[0].wait()


def payload_kernel(high_ref, low_ref, tok_ref, padding_ref, out_a_ref, out_b_ref):
    samples, span, _ = high_ref.shape
    rows = tok_ref.shape[0]
    atoms = rows * span
    index = lax.broadcasted_iota(jnp.int32, (CODE_ROWS, span), 0)
    place = lax.broadcasted_iota(jnp.int32, (1, span), 1)

    def write(out_ref, act_ref, row):
        for s in range(samples):
            out_ref[s * span : (s + 1) * span, :] = act_ref[s]
        live = place + row * span < atoms - padding_ref[0]
        code = jnp.where(live, tok_ref[row : row + 1, :] + 1, 0)
        top, low = code // CODE_BASE, code % CODE_BASE
        both = jnp.where(index == 0, top, jnp.where(index == 1, low, 0))
        out_ref[samples * span :, :] = both.astype(F32).astype(BF16)

    is_odd = lax.axis_index("atoms") % 2 == 1

    @pl.when(is_odd)
    def _():
        write(out_a_ref, low_ref, 0)
        write(out_b_ref, high_ref, rows - 1)

    @pl.when(jnp.logical_not(is_odd))
    def _():
        write(out_a_ref, high_ref, rows - 1)
        write(out_b_ref, low_ref, 0)


def attention_kernel(geo, sides, edge, chained, last, *refs):
    samples, atoms, channels, heads, win_rows, span, cp, out_half = geo
    refs = list(refs)
    take = lambda n: [refs.pop(0) for _ in range(n)]
    offsets_ref, padding_ref, wtok_ref = take(3)
    tok_ref, act_hbm, gout_hbm, pair_hbm = take(4)
    wq_ref, wk_ref, wv_ref, wg_ref, wo_ref, wpair_ref = take(6)
    if edge:
        halo_a, halo_b = take(2)
    if chained:
        (acc_in_ref,) = take(1)
    ga_refs = take(len(sides))
    if edge:
        ga_out_refs = take(2)
    if last:
        acc_mine_ref, acc_other_ref = take(2)
    else:
        (acc_ref,) = take(1)
    mine_ref, other_ref = take(2)
    pair_ref, pair_sem, wexp_ref, pw_ref, code_ref, qcode_ref, halo_code_ref = take(7)
    act_ref, gout_ref, in_sem, q_ref, datt_ref, g_ref, gy_ref = take(7)
    dq_ref, dgate_ref, gated_ref, bias_ref, bsum_ref = take(5)
    if last:
        (acc_ref,) = take(1)
    if edge:
        ga_halo_ref, ga_sem = take(2)
    n_blocks = len(sides) * samples
    k_refs = take(n_blocks)
    v_refs = take(n_blocks)
    dk_refs = take(n_blocks)
    dv_refs = take(n_blocks)

    half_rows = win_rows // 2
    head_dim = channels // heads
    scale = 1.0 / math.sqrt(head_dim)
    rank = lax.axis_index("atoms")
    core = lax.axis_index("samples")
    anchor = rank * atoms
    all_atoms = lax.axis_size("atoms") * atoms
    odd = rank % 2
    is_odd = odd == 1

    def halo_copy(source, row, rows, target, sem):
        refs = (halo_a, halo_b) if source == "lo" else (halo_b, halo_a)
        return HaloCopy(is_odd, *[ref.at[pl.ds(row, rows)] for ref in refs], target, sem)


    block_copies = []
    for n, side in enumerate(sides):
        for s in range(samples):
            block = n * samples + s
            mine = []
            for i, (source, row, rows, at) in enumerate(side.pieces):
                target, sem = act_ref.at[block, pl.ds(at, rows)], in_sem.at[block, i]
                if source == "act":
                    mine.append(
                        pltpu.make_async_copy(act_hbm.at[s, pl.ds(row, rows)], target, sem)
                    )
                else:
                    mine.append(halo_copy(source, s * span, rows, target, sem))
            mine.append(
                pltpu.make_async_copy(
                    gout_hbm.at[s, pl.ds(side.query_row, side.queries)],
                    gout_ref.at[block],
                    in_sem.at[block, 2],
                )
            )
            block_copies.append(mine)
    code_copies = []
    if edge:
        for i, source in enumerate(("lo", "hi")):
            code_copies.append(
                halo_copy(
                    source,
                    samples * span,
                    CODE_ROWS,
                    halo_code_ref.at[i],
                    pair_sem.at[len(sides) + i],
                )
            )
    pair_copies = []
    first = 0
    for n, side in enumerate(sides):
        pair_copies.append(
            pltpu.make_async_copy(
                pair_hbm.at[pl.ds(side.first, side.count)],
                pair_ref.at[pl.ds(first, side.count)],
                pair_sem.at[n],
            )
        )
        first += side.count
    for copy in code_copies:
        copy.start()
    for copies in block_copies:
        for copy in copies:
            copy.start()
    for copy in pair_copies:
        copy.start()

    lane = lax.broadcasted_iota(jnp.int32, (1, channels), 1)
    head_masks = [(lane // head_dim == h).astype(F32) for h in range(heads)]
    head_masks_b = [m.astype(BF16) for m in head_masks]

    lanes = 2 * heads * half_rows
    s_lane = lax.broadcasted_iota(jnp.int32, (1, lanes), 1)
    lane_head = (s_lane // half_rows) % heads
    lane_row = (s_lane // (heads * half_rows)) * half_rows + s_lane % half_rows
    wtok = jnp.zeros((1, lanes), F32)
    for h in range(heads):
        wtok = jnp.where(lane_head == h, wtok_ref[h], wtok)
    pick = (
        lax.broadcasted_iota(jnp.int32, (heads, lanes), 0)
        == (lax.broadcasted_iota(jnp.int32, (heads, lanes), 1) // half_rows) % heads
    ).astype(BF16)
    wlane = dot_tn(wpair_ref[...], pick).astype(BF16)
    for i in range(win_rows):
        wexp_ref[i * cp : (i + 1) * cp, :] = jnp.where(lane_row == i, wlane, 0.0).astype(BF16)
    pw_ref[...] = jnp.zeros_like(pw_ref)

    per_row = span // win_rows
    code = tok_ref[...] + 1
    top = (code // CODE_BASE).astype(F32).astype(BF16)
    low = (code % CODE_BASE).astype(F32).astype(BF16)
    source_lane = lax.broadcasted_iota(jnp.int32, (span, lanes), 0)
    for m in range(per_row):
        spread = (source_lane == m * win_rows + lane_row).astype(F32).astype(BF16)
        qcode_ref[m, : code.shape[0], :] = dot(top, spread) * CODE_BASE + dot(low, spread)

    live = jnp.where(
        lax.broadcasted_iota(jnp.int32, code.shape, 0) * span
        + lax.broadcasted_iota(jnp.int32, code.shape, 1)
        < atoms - padding_ref[0],
        code,
        0,
    ).astype(F32)
    for r in range(code.shape[0]):
        if any(
            r * span < row + rows and row < (r + 1) * span
            for side in sides
            for source, row, rows, _ in side.pieces
            if source == "act"
        ):
            code_ref[(r + 1) * span : (r + 2) * span, :] = column_of(live[r : r + 1], span)
    for copy in code_copies:
        copy.wait()
    if edge:
        for i, at in enumerate((0, atoms + span)):
            two = halo_code_ref[i].astype(F32)
            row = two[0:1, :] * CODE_BASE + two[1:2, :]
            code_ref[at : at + span, :] = column_of(row, span)

    w_kv = jnp.concatenate([wk_ref[...], wv_ref[...]], axis=1)
    w_qg = jnp.concatenate([wq_ref[...], wg_ref[...]], axis=1)
    for n, side in enumerate(sides):
        for s in range(samples):
            block = n * samples + s
            for copy in block_copies[block]:
                copy.wait()
            kv = dot(act_ref[block], w_kv)
            k_refs[block][...] = kv[:, :channels]
            v_refs[block][...] = kv[:, channels:]
            dk_refs[block][...] = jnp.zeros_like(dk_refs[block])
            dv_refs[block][...] = jnp.zeros_like(dv_refs[block])
            at = side.query_row - side.origin
            qg = dot(act_ref[block, at : at + side.queries, :], w_qg)
            q_ref[block] = qg[:, :channels].astype(BF16)
            gate = jax.nn.sigmoid(qg[:, channels:])
            gy = dot_nt(gout_ref[block], wo_ref[...])
            g_ref[block] = gate
            gy_ref[block] = gy
            datt_ref[block] = (gy * gate).astype(BF16)

    for copy in pair_copies:
        copy.wait()

    def by_head(rows):
        return jnp.concatenate(
            [
                rows[half * half_rows : (half + 1) * half_rows] * head_masks_b[h]
                for half in range(2)
                for h in range(heads)
            ],
            axis=0,
        )

    def own_head(wide):
        halves = []
        for half in range(2):
            total = None
            for h in range(heads):
                at = (half * heads + h) * half_rows
                term = wide[at : at + half_rows] * head_masks[h]
                total = term if total is None else total + term
            halves.append(total)
        return jnp.concatenate(halves, axis=0)

    def window_group(members, w, tok_sum):
        keys, qrows, same, pair_w = [], [], [], []
        for lane_slot, (n, side, first, shift) in enumerate(members):
            window = side.first + shift + w
            start = jnp.clip(
                anchor + window * win_rows + offsets_ref[window], 0, all_atoms - span
            ) - (anchor + side.origin)
            start = jnp.clip(start, 0, side.rows - span)
            key_codes = code_ref[pl.ds(start + (side.origin + span), span), :]
            query_codes = qcode_ref[window % per_row, pl.ds(window // per_row, 1), :]
            same.append(key_codes == query_codes)
            pair_w.append(pair_ref.at[first + shift + w])
            bias = dot_tn(pair_w[-1][...], wexp_ref[...]) + jnp.where(same[-1], wtok, 0.0)
            bias_ref[lane_slot] = jnp.where(key_codes > 0.0, bias, MASKED) * LOG2E
            at = pl.multiple_of((shift + w) * win_rows, win_rows)
            qrows.append(pl.ds(at, win_rows))
            keys.append(pl.ds(start, span))

        def products(m, s):
            block = members[m][0] * samples + s
            kb = k_refs[block][keys[m], :].astype(BF16)
            vb = v_refs[block][keys[m], :].astype(BF16)
            qh = by_head(q_ref[block, qrows[m], :])
            dh = by_head(datt_ref[block, qrows[m], :])
            return kb, vb, qh, dh, dot_nt(kb, qh), dot_nt(vb, dh)

        def softmax(m, state):
            kb, vb, qh, dh, x, dp = state
            x = x * (scale * LOG2E) + bias_ref[m]
            e = jnp.exp2(x - jnp.max(x, axis=0, keepdims=True))
            p = e * (1.0 / jnp.sum(e, axis=0, keepdims=True))
            t = p * dp
            ds = t - p * jnp.sum(t, axis=0, keepdims=True)
            return kb, vb, qh, dh, p.astype(BF16), ds

        def gradients(m, s, state):
            block = members[m][0] * samples + s
            kb, vb, qh, dh, pb, ds = state
            dsb = ds.astype(BF16)
            if s == 0:
                bsum_ref[m] = ds
            else:
                bsum_ref[m] += ds
            dk_refs[block][keys[m], :] += dot(dsb, qh)
            dv_refs[block][keys[m], :] += dot(pb, dh)
            att = own_head(dot_tn(pb, vb))
            rows = qrows[m]
            dq_ref[block, rows, :] = (own_head(dot_tn(dsb, kb)) * scale).astype(BF16)
            gate = g_ref[block, rows, :]
            ga = gate * att
            gated_ref[block, rows, :] = ga.astype(BF16)
            dgate_ref[block, rows, :] = (gy_ref[block, rows, :] * ga * (1.0 - gate)).astype(BF16)

        order = [(m, s) for s in range(samples) for m in range(len(members))]
        states = [products(m, s) for m, s in order]
        states = [softmax(m, state) for (m, _), state in zip(order, states)]
        for (m, s), state in zip(order, states):
            gradients(m, s, state)
        width = heads * half_rows
        for m, (n, side, first, shift) in enumerate(members):
            total = bsum_ref[m]
            pw_ref[...] += dot(pair_w[m][...], total.astype(BF16))
            tok_sum += jnp.sum(jnp.where(same[m], total, 0.0), axis=0, keepdims=True)
            bsum_ref[m] = total.T
            slot = first + shift + w
            mine_ref[slot] = bsum_ref[m, pl.ds(pl.multiple_of(core * width, width), width), :]
            other_ref[slot] = bsum_ref[
                m, pl.ds(pl.multiple_of((1 - core) * width, width), width), :
            ].astype(BF16)
        return tok_sum

    tok_sum = jnp.zeros((1, lanes), F32)
    if len(sides) == 2:
        members = [(0, sides[0], 0, 0), (1, sides[1], sides[0].count, 0)]
        tok_sum = lax.fori_loop(
            0, sides[0].count, functools.partial(window_group, members), tok_sum
        )
    else:
        half = sides[0].count // 2
        members = [(0, sides[0], 0, 0), (0, sides[0], 0, half)]
        tok_sum = lax.fori_loop(0, half, functools.partial(window_group, members), tok_sum)
        if sides[0].count % 2:
            rest = [(0, sides[0], 0, sides[0].count - 1)]
            tok_sum = window_group(rest, 0, tok_sum)

    pending = []
    acc_kv = jnp.zeros((channels, 2 * channels), F32)
    acc_qg = jnp.zeros((channels, 2 * channels), F32)
    acc_o = jnp.zeros((channels, channels), F32)
    for n, side in enumerate(sides):
        at = side.query_row - side.origin
        for s in range(samples):
            block = n * samples + s
            dkv_b = jnp.concatenate(
                [(dk_refs[block][...] * scale).astype(BF16), dv_refs[block][...].astype(BF16)],
                axis=1,
            )
            dqg = jnp.concatenate([dq_ref[block], dgate_ref[block]], axis=1)
            part = dot_nt(dkv_b, w_kv)
            middle = part[at : at + side.queries] + dot_nt(dqg, w_qg)
            runs = [(0, part[:at]), (at, middle), (at + side.queries, part[at + side.queries :])]
            for run_at, run in runs:
                if run.shape[0] == 0:
                    continue
                run = run.astype(BF16)
                for source, _, rows, piece_at in side.pieces:
                    low = max(run_at, piece_at)
                    high = min(run_at + run.shape[0], piece_at + rows)
                    if low >= high:
                        continue
                    value = run[low - run_at : high - run_at]
                    if source == "lo":
                        ga_halo_ref[1 - odd, s, low - piece_at : high - piece_at, :] = value
                    elif source == "hi":
                        ga_halo_ref[odd, s, low - piece_at : high - piece_at, :] = value
                    else:
                        ga_refs[n][s, low - piece_at : high - piece_at, :] = value
            pending.append((dkv_b, dqg))
    ga_copies = []
    if edge:
        for i, out_ref in enumerate(ga_out_refs):
            ga_copies.append(pltpu.make_async_copy(ga_halo_ref.at[i], out_ref, ga_sem.at[i]))
            ga_copies[-1].start()
    for n, side in enumerate(sides):
        at = side.query_row - side.origin
        for s in range(samples):
            block = n * samples + s
            dkv_b, dqg = pending[block]
            acc_kv = acc_kv + dot_tn(act_ref[block], dkv_b)
            acc_qg = acc_qg + dot_tn(act_ref[block, at : at + side.queries, :], dqg)
            acc_o = acc_o + dot_tn(gated_ref[block], gout_ref[block])

    diag = lax.broadcasted_iota(jnp.int32, (win_rows * cp, lanes), 0) // cp == lane_row
    pw = jnp.where(diag, pw_ref[...], 0.0).reshape(win_rows, cp, lanes).sum(axis=0)
    parts = [
        acc_qg[:, :channels],
        acc_kv[:, :channels],
        acc_kv[:, channels:],
        acc_qg[:, channels:],
        acc_o,
    ]
    first_half, second_half = [], []
    left = out_half
    for part in parts:
        if left >= channels:
            first_half.append(part)
            left -= channels
        elif left > 0:
            first_half.append(part[:left])
            second_half.append(part[left:])
            left = 0
        else:
            second_half.append(part)
    tok_rows = jnp.where(
        lax.broadcasted_iota(jnp.int32, (SMALL_ROWS, lanes), 0) == 0, tok_sum, 0.0
    )
    for half, group in enumerate((first_half + [pw], second_half + [tok_rows])):
        at = 0
        for part in group:
            rows = part.shape[0]
            if chained:
                part = part + acc_in_ref[half, at : at + rows, :]
            acc_ref[half, at : at + rows, :] = part
            at += rows
    for copy in ga_copies:
        copy.wait()
    if last:
        acc_mine_ref[...] = acc_ref[core]
        value = acc_ref[1 - core]
        wide = value.shape[0] - SMALL_ROWS
        top = value.astype(BF16)
        acc_other_ref[: wide + SMALL_ROWS, :] = top
        rest = value[wide:] - top[wide:].astype(F32)
        acc_other_ref[wide + SMALL_ROWS :, :] = rest.astype(BF16)


def pair_kernel(wpair_ref, *refs, order, heads, cp):
    out_ref = refs[-1]
    rows = refs[0].shape[1]
    half_rows = rows // heads
    lane = lax.broadcasted_iota(jnp.int32, (1, rows), 1)
    pick = (
        lax.broadcasted_iota(jnp.int32, (heads, rows), 0)
        == lax.broadcasted_iota(jnp.int32, (heads, rows), 1) // half_rows
    ).astype(BF16)
    wlane = dot_tn(wpair_ref[...], pick)
    wexp = jnp.concatenate(
        [jnp.where(lane % half_rows == i, wlane, 0.0) for i in range(half_rows)], axis=0
    ).astype(BF16)
    for which, group in enumerate(order):
        m_ref, r_ref = refs[2 * which], refs[2 * which + 1]
        for slot, window in enumerate(group):
            total = (m_ref[slot] + r_ref[slot].astype(F32)).astype(BF16)
            out_ref[window] = dot(wexp, total).astype(BF16)


def act_sum_kernel(firsts, *refs):
    out_ref = refs[-1]
    atoms = out_ref.shape[1]
    is_odd = lax.axis_index("atoms") % 2 == 1
    from_a, from_b = refs[-3][...].astype(F32), refs[-2][...].astype(F32)
    halos = [jnp.where(is_odd, from_a, from_b), jnp.where(is_odd, from_b, from_a)]
    span = from_a.shape[1]
    halo_rows = [(0, halos[0]), (atoms - span, halos[1])]
    marks = {0, span, atoms - span, atoms}
    for first, ref in zip(firsts, refs):
        marks |= {first, first + ref.shape[1]}
    marks = sorted(marks)
    for low, high in zip(marks[:-1], marks[1:]):
        total = None
        for first, halo in halo_rows:
            if first <= low and high <= first + span:
                total = halo[:, low - first : high - first]
        for first, ref in zip(firsts, refs):
            if first <= low and high <= first + ref.shape[1]:
                term = ref[:, low - first : high - first, :].astype(F32)
                total = term if total is None else total + term
        out_ref[:, low:high, :] = total.astype(BF16)


def finish_kernel(sent_ref, got_ref, gw_ref, gpw_ref, gtok_ref, *, heads):
    rows = sent_ref.shape[0]
    wide = rows - 2 * SMALL_ROWS
    channels = gw_ref.shape[1]
    is_first = lax.axis_index("samples") == 0
    sent, got = sent_ref[...].astype(F32), got_ref[...].astype(F32)
    first = jnp.where(is_first, sent, got)
    second = jnp.where(is_first, got, sent)
    gw_ref[:wide, :] = first[:wide]
    gw_ref[wide:, :] = second[:wide]
    pw = first[wide : wide + SMALL_ROWS] + first[wide + SMALL_ROWS :]
    tok = second[wide : wide + 1] + second[wide + SMALL_ROWS : wide + SMALL_ROWS + 1]
    half_rows = channels // (2 * heads)
    head = (lax.broadcasted_iota(jnp.int32, (heads, channels), 1) // half_rows) % heads
    pick = (head == lax.broadcasted_iota(jnp.int32, (heads, channels), 0)).astype(F32)
    gpw_ref[...] = lax.dot_general(
        pick,
        pw,
        (((1,), (1,)), ((), ())),
        precision=lax.Precision.HIGHEST,
        preferred_element_type=F32,
    )
    for h in range(heads):
        gtok_ref[h] = jnp.sum(tok * pick[h : h + 1])


def per_device(
    act,
    grad_out,
    pair,
    w_query,
    w_key,
    w_value,
    w_gate,
    w_out,
    w_pair,
    w_token,
    offsets,
    atom_token,
    padding,
):
    samples, atoms, channels = act.shape
    windows = offsets.shape[0]
    win_rows = atoms // windows
    span = pair.shape[-1]
    cp, heads = w_pair.shape
    half_rows = win_rows // 2
    lanes = heads * win_rows
    ranges = lax.axis_size("atoms")
    cores = lax.axis_size("samples")
    assert cores == 2 and ranges & (ranges - 1) == 0
    tok = atom_token.reshape(atoms // span, span)
    w_pair_t = w_pair.T
    vmem = pl.BlockSpec(memory_space=pltpu.VMEM)
    smem = pl.BlockSpec(memory_space=pltpu.SMEM)
    hbm = pl.BlockSpec(memory_space=pl.ANY)

    exchanges = [
        [pair for i in range(first, ranges - 1, 2) for pair in ((i, i + 1), (i + 1, i))]
        for first in range(2)
    ]
    last_block = atoms // span - 1
    to_send = pl.pallas_call(
        payload_kernel,
        out_shape=[jax.ShapeDtypeStruct((samples * span + CODE_ROWS, channels), BF16)] * 2,
        grid=(1,),
        in_specs=[
            pl.BlockSpec((samples, span, channels), lambda i: (0, last_block, 0)),
            pl.BlockSpec((samples, span, channels), lambda i: (0, 0, 0)),
            vmem,
            smem,
        ],
        out_specs=[vmem, vmem],
    )(act, act, tok, padding)
    halos = [lax.ppermute(part, "atoms", swaps) for part, swaps in zip(to_send, exchanges)]

    out_half = 5 * channels // 2
    part_rows = out_half + SMALL_ROWS
    coded_rows = part_rows + SMALL_ROWS
    geo = (samples, atoms, channels, heads, win_rows, span, cp, out_half)
    pair_flat = pair.reshape(windows, win_rows * cp, span)
    width = heads * half_rows
    common = (
        offsets,
        padding,
        w_token,
        tok,
        act,
        grad_out,
        pair_flat,
        w_query,
        w_key,
        w_value,
        w_gate,
        w_out,
        w_pair_t,
    )
    shape = jax.ShapeDtypeStruct

    def call(sides, halos=(), acc_in=None, last=False):
        edge, chained = len(halos) > 0, acc_in is not None
        args = common + tuple(halos) + ((acc_in,) if chained else ())
        in_specs = [smem] * 3 + [vmem] + [hbm] * 3 + [vmem] * 6 + [hbm] * len(halos)
        in_specs += [vmem] * chained
        count = sum(side.count for side in sides)
        queries, rows = sides[0].queries, sides[0].rows
        blocks = len(sides) * samples
        own_rows = [sum(p[2] for p in side.pieces if p[0] == "act") for side in sides]
        out_shape = [shape((samples, n, channels), BF16) for n in own_rows]
        if edge:
            out_shape += [shape((samples, span, channels), BF16)] * 2
        if last:
            out_shape += [shape((part_rows, channels), F32), shape((coded_rows, channels), BF16)]
        else:
            out_shape += [shape((2, part_rows, channels), F32)]
        out_specs = [vmem] * (len(out_shape) + 2)
        if edge:
            at = len(own_rows)
            out_specs[at : at + 2] = [hbm] * 2
        out_shape += [shape((count, width, span), F32), shape((count, width, span), BF16)]
        per_query = (blocks, queries, channels)
        scratch = [
            pltpu.VMEM((count, win_rows * cp, span), BF16),
            pltpu.SemaphoreType.DMA((len(sides) + 2,)),
            pltpu.VMEM((win_rows * cp, lanes), BF16),
            pltpu.VMEM((win_rows * cp, lanes), F32),
            pltpu.VMEM((atoms + 2 * span, span), F32),
            pltpu.VMEM((span // win_rows, -(-atoms // span // 8) * 8, lanes), F32),
            pltpu.VMEM((2, CODE_ROWS, span), BF16),
            pltpu.VMEM((blocks, rows, channels), BF16),
            pltpu.VMEM(per_query, BF16),
            pltpu.SemaphoreType.DMA((blocks, 3)),
            pltpu.VMEM(per_query, BF16),
            pltpu.VMEM(per_query, BF16),
            pltpu.VMEM(per_query, F32),
            pltpu.VMEM(per_query, F32),
            pltpu.VMEM(per_query, BF16),
            pltpu.VMEM(per_query, BF16),
            pltpu.VMEM(per_query, BF16),
            pltpu.VMEM((2, span, lanes), F32),
            pltpu.VMEM((2, span, lanes), F32),
        ]
        if last:
            scratch += [pltpu.VMEM((2, part_rows, channels), F32)]
        if edge:
            scratch += [
                pltpu.VMEM((2, samples, span, channels), BF16),
                pltpu.SemaphoreType.DMA((2,)),
            ]
        scratch += [pltpu.VMEM((rows, channels), F32)] * (4 * blocks)
        units = 6 * count * samples + 8 * count + 14 * blocks
        return pl.pallas_call(
            functools.partial(attention_kernel, geo, sides, edge, chained, last),
            out_shape=out_shape,
            in_specs=in_specs,
            out_specs=out_specs,
            scratch_shapes=scratch,
            compiler_params=pltpu.CompilerParams(vmem_limit_bytes=VMEM_LIMIT),
            cost_estimate=pl.CostEstimate(
                flops=2 * units * 128 * 128 * 128 * 4,
                bytes_accessed=12_000_000,
                transcendentals=count * samples * span * lanes,
            ),
        )(*args)

    edge_count = span // win_rows
    early_count = (windows - 2 * edge_count) * EARLY_SHARE // 12
    early = tuple(range(edge_count, edge_count + early_count))
    late = tuple(range(edge_count + early_count, windows - edge_count))
    low, high = tuple(range(edge_count)), tuple(range(windows - edge_count, windows))
    early_end = (early[-1] + 1) * win_rows + span
    late_first = late[0] * win_rows - span
    own = edge_count * win_rows + span
    swap = [(0, 1), (1, 0)]

    early_side = Side(early, win_rows, early_end, [("act", 0, early_end, 0)], 0)
    ga_early, acc, mine1, other1 = call([early_side])
    recv1 = lax.ppermute(other1, "samples", swap)

    low_side = Side(low, win_rows, own + span, [("lo", 0, span, 0), ("act", 0, own, span)], -span)
    high_side = Side(
        high,
        win_rows,
        own + span,
        [("act", atoms - own, own, 0), ("hi", 0, span, own)],
        atoms - own,
    )
    ga_low, ga_high, ga_a, ga_b, acc, mine2, other2 = call([low_side, high_side], halos, acc)
    recv2 = lax.ppermute(other2, "samples", swap)
    from_a, from_b = [
        lax.ppermute(part, "atoms", swaps) for part, swaps in zip((ga_a, ga_b), exchanges)
    ]

    late_rows = atoms - late_first
    late_side = Side(
        late, win_rows, late_rows, [("act", late_first, late_rows, 0)], late_first
    )
    ga_late, acc_mine, acc_other, mine3, other3 = call([late_side], (), acc, True)

    wide = out_half

    def encode(value):
        top = lax.reduce_precision(value, 8, 7)
        return jnp.concatenate([top, value[wide:] - top[wide:]]).astype(BF16)

    def decode(sent):
        sent = sent.astype(F32)
        return jnp.concatenate(
            [sent[:wide], sent[wide : wide + SMALL_ROWS] + sent[wide + SMALL_ROWS :]]
        )

    acc_other, other3, from_a, from_b = lax.optimization_barrier(
        (acc_other, other3, from_a, from_b)
    )
    recv3 = lax.ppermute(other3, "samples", swap)
    total = acc_mine + decode(lax.ppermute(acc_other, "samples", swap))
    grad_pair = pl.pallas_call(
        functools.partial(pair_kernel, order=(early, low + high, late), heads=heads, cp=cp),
        out_shape=shape((windows, half_rows * cp, span), BF16),
        in_specs=[vmem] * 7,
        out_specs=vmem,
        compiler_params=pltpu.CompilerParams(vmem_limit_bytes=VMEM_LIMIT),
        cost_estimate=pl.CostEstimate(
            flops=2 * windows * 256 * 256 * 256, bytes_accessed=4_000_000, transcendentals=0
        ),
    )(w_pair_t, mine1, recv1, mine2, recv2, mine3, recv3)

    pieces = [
        (0, ga_early),
        (late_first, ga_late),
        (0, ga_low),
        (atoms - own, ga_high),
    ]
    parts = [part for _, part in pieces] + [from_a, from_b]
    grad_act = pl.pallas_call(
        functools.partial(act_sum_kernel, [first for first, _ in pieces]),
        out_shape=shape((samples, atoms, channels), BF16),
        grid=(2,),
        in_specs=[
            pl.BlockSpec((samples // 2,) + part.shape[1:], lambda s: (s, 0, 0))
            for part in parts
        ],
        out_specs=pl.BlockSpec((samples // 2, atoms, channels), lambda s: (s, 0, 0)),
        compiler_params=pltpu.CompilerParams(vmem_limit_bytes=VMEM_LIMIT),
        cost_estimate=pl.CostEstimate(
            flops=4 * samples * atoms * channels, bytes_accessed=6_000_000, transcendentals=0
        ),
    )(*parts)
    step = ranges // 2
    while step >= 1:
        if step == ranges // 4:
            total, grad_pair = lax.optimization_barrier((total, grad_pair))
        if step == ranges // 8:
            total, grad_act = lax.optimization_barrier((total, grad_act))
        sent = encode(total)
        got = lax.ppermute(sent, "atoms", [(i, i ^ step) for i in range(ranges)])
        total = decode(sent) + decode(got)
        step //= 2
    sent = encode(total)
    got = lax.ppermute(sent, "samples", swap)
    grad_weights, grad_pair_weight, grad_token_weight = pl.pallas_call(
        functools.partial(finish_kernel, heads=heads),
        out_shape=[
            shape((5 * channels, channels), F32),
            shape((heads, cp), F32),
            shape((heads,), F32),
        ],
        in_specs=[vmem, vmem],
        out_specs=[vmem, vmem, smem],
    )(sent, got)

    return (
        grad_act,
        grad_pair.reshape(windows, half_rows, cp, span),
        grad_weights.reshape(5, channels, channels),
        grad_pair_weight.T,
        grad_token_weight,
    )


def solution(mesh):
    in_specs = (
        P("samples", ("groups", "atoms"), None),
        P("samples", ("groups", "atoms"), None),
        P(("groups", "atoms"), None, None, None),
        P(),
        P(),
        P(),
        P(),
        P(),
        P(),
        P(),
        P(("groups", "atoms")),
        P(("groups", "atoms")),
        P(("groups", "atoms")),
    )
    out_specs = (
        P("samples", ("groups", "atoms"), None),
        P(("groups", "atoms"), "samples", None, None),
        P("groups", None, None),
        P("groups", None),
        P("groups"),
    )
    return jax.shard_map(
        per_device, mesh=mesh, in_specs=in_specs, out_specs=out_specs, check_vma=False
    )
```

```python
import functools
import math

import jax
import jax.numpy as jnp
from jax import lax
from jax.experimental import pallas as pl
from jax.experimental.pallas import tpu as pltpu
from jax.sharding import PartitionSpec as P

BF16 = jnp.bfloat16
F32 = jnp.float32
MASKED = -1000000000.0
LOG2E = math.log2(math.e)
CODE_ROWS = 16
CODE_BASE = 128
SMALL_ROWS = 16
VMEM_LIMIT = 56 * 1024 * 1024
EARLY_SHARE = 6


def dot(a, b):
    return lax.dot_general(a, b, (((1,), (0,)), ((), ())), preferred_element_type=F32)


def dot_nt(a, b):
    return lax.dot_general(a, b, (((1,), (1,)), ((), ())), preferred_element_type=F32)


def dot_tn(a, b):
    return lax.dot_general(a, b, (((0,), (0,)), ((), ())), preferred_element_type=F32)


def column_of(row, span):
    return jnp.broadcast_to(row, (span, row.shape[-1])).T


class Side:
    def __init__(self, windows, win_rows, rows, pieces, origin):
        self.first = windows[0]
        self.count = len(windows)
        self.queries = len(windows) * win_rows
        self.query_row = windows[0] * win_rows
        self.rows = rows
        self.pieces = pieces
        self.origin = origin


class HaloCopy:
    def __init__(self, is_odd, when_odd, when_even, target, sem):
        self.is_odd = is_odd
        self.options = [pltpu.make_async_copy(s, target, sem) for s in (when_even, when_odd)]

    def start(self):
        pl.when(self.is_odd)(self.options[1].start)
        pl.when(jnp.logical_not(self.is_odd))(self.options[0].start)

    def wait(self):
        self.options[0].wait()


def payload_kernel(high_ref, low_ref, tok_ref, padding_ref, out_a_ref, out_b_ref):
    samples, span, _ = high_ref.shape
    rows = tok_ref.shape[0]
    atoms = rows * span
    index = lax.broadcasted_iota(jnp.int32, (span, span), 0)
    place = lax.broadcasted_iota(jnp.int32, (1, span), 1)

    def write(out_ref, act_ref, row):
        out_ref[:samples] = act_ref[...]
        live = place + row * span < atoms - padding_ref[0]
        code = jnp.where(live, tok_ref[row : row + 1, :] + 1, 0)
        top, low = code // CODE_BASE, code % CODE_BASE
        both = jnp.where(index == 0, top, jnp.where(index == 1, low, 0))
        out_ref[samples] = both.astype(F32).astype(BF16)

    is_odd = lax.axis_index("atoms") % 2 == 1

    @pl.when(is_odd)
    def _():
        write(out_a_ref, low_ref, 0)
        write(out_b_ref, high_ref, rows - 1)

    @pl.when(jnp.logical_not(is_odd))
    def _():
        write(out_a_ref, high_ref, rows - 1)
        write(out_b_ref, low_ref, 0)


def attention_kernel(geo, sides, edge, chained, last, *refs):
    samples, atoms, channels, heads, win_rows, span, cp, out_half = geo
    refs = list(refs)
    take = lambda n: [refs.pop(0) for _ in range(n)]
    offsets_ref, padding_ref, wtok_ref = take(3)
    tok_ref, act_hbm, gout_hbm, pair_hbm = take(4)
    wq_ref, wk_ref, wv_ref, wg_ref, wo_ref, wpair_ref = take(6)
    if edge:
        halo_a, halo_b = take(2)
    if chained:
        (acc_in_ref,) = take(1)
    ga_hbm = take(len(sides))
    if edge:
        ga_out_refs = take(2)
    if last:
        acc_mine_ref, acc_other_ref = take(2)
    else:
        (acc_ref,) = take(1)
    mine_hbm, other_hbm = take(2)
    pair_ref, pair_sem, wexp_ref, pw_ref, code_ref, qcode_ref, halo_code_ref = take(7)
    act_ref, gout_ref, in_sem, q_ref, datt_ref, g_ref, gy_ref = take(7)
    dq_ref, dgate_ref, gated_ref, bias_ref, bsum_ref = take(5)
    if last:
        (acc_ref,) = take(1)
    if edge:
        (ga_halo_ref,) = take(1)
    ga_refs = take(len(sides))
    mine_ref, other_ref, out_sem = take(3)
    n_blocks = len(sides) * samples
    k_refs = take(n_blocks)
    v_refs = take(n_blocks)
    dk_refs = take(n_blocks)
    dv_refs = take(n_blocks)

    half_rows = win_rows // 2
    head_dim = channels // heads
    scale = 1.0 / math.sqrt(head_dim)
    rank = lax.axis_index("atoms")
    core = lax.axis_index("samples")
    anchor = rank * atoms
    all_atoms = lax.axis_size("atoms") * atoms
    odd = rank % 2
    is_odd = odd == 1

    def halo_copy(source, place, target, sem):
        refs = (halo_a, halo_b) if source == "lo" else (halo_b, halo_a)
        return HaloCopy(is_odd, *[ref.at[place] for ref in refs], target, sem)


    part = samples // 2
    part_copies = {}
    for n, side in enumerate(sides):
        for s in range(0, samples, part):
            run = pl.ds(s, part)
            block_run = pl.ds(n * samples + s, part)
            mine = []
            for i, (source, row, rows, at) in enumerate(side.pieces):
                target, sem = act_ref.at[block_run, pl.ds(at, rows)], in_sem.at[n, s // part, i]
                if source == "act":
                    mine.append(
                        pltpu.make_async_copy(act_hbm.at[run, pl.ds(row, rows)], target, sem)
                    )
                else:
                    mine.append(halo_copy(source, run, target, sem))
            mine.append(
                pltpu.make_async_copy(
                    gout_hbm.at[run, pl.ds(side.query_row, side.queries)],
                    gout_ref.at[block_run],
                    in_sem.at[n, s // part, 2],
                )
            )
            part_copies[n, s] = mine
    code_copies = []
    if edge:
        for i, source in enumerate(("lo", "hi")):
            code_copies.append(
                halo_copy(
                    source,
                    (samples, pl.ds(0, CODE_ROWS)),
                    halo_code_ref.at[i],
                    pair_sem.at[len(sides) + i],
                )
            )
    pair_copies = []
    first = 0
    for n, side in enumerate(sides):
        pair_copies.append(
            pltpu.make_async_copy(
                pair_hbm.at[pl.ds(side.first, side.count)],
                pair_ref.at[pl.ds(first, side.count)],
                pair_sem.at[n],
            )
        )
        first += side.count
    for copy in code_copies:
        copy.start()
    for copies in part_copies.values():
        for copy in copies:
            copy.start()
    for copy in pair_copies:
        copy.start()

    lane = lax.broadcasted_iota(jnp.int32, (1, channels), 1)
    head_masks = [(lane // head_dim == h).astype(F32) for h in range(heads)]
    head_masks_b = [m.astype(BF16) for m in head_masks]

    lanes = 2 * heads * half_rows
    s_lane = lax.broadcasted_iota(jnp.int32, (1, lanes), 1)
    lane_head = (s_lane // half_rows) % heads
    lane_row = (s_lane // (heads * half_rows)) * half_rows + s_lane % half_rows
    wtok = jnp.zeros((1, lanes), F32)
    for h in range(heads):
        wtok = jnp.where(lane_head == h, wtok_ref[h], wtok)
    pick = (
        lax.broadcasted_iota(jnp.int32, (heads, lanes), 0)
        == (lax.broadcasted_iota(jnp.int32, (heads, lanes), 1) // half_rows) % heads
    ).astype(BF16)
    wlane = dot_tn(wpair_ref[...], pick).astype(BF16)
    for i in range(win_rows):
        wexp_ref[i * cp : (i + 1) * cp, :] = jnp.where(lane_row == i, wlane, 0.0).astype(BF16)
    pw_ref[...] = jnp.zeros_like(pw_ref)

    per_row = span // win_rows
    code = tok_ref[...] + 1
    top = (code // CODE_BASE).astype(F32).astype(BF16)
    low = (code % CODE_BASE).astype(F32).astype(BF16)
    source_lane = lax.broadcasted_iota(jnp.int32, (span, lanes), 0)
    for m in range(per_row):
        spread = (source_lane == m * win_rows + lane_row).astype(F32).astype(BF16)
        qcode_ref[m, : code.shape[0], :] = dot(top, spread) * CODE_BASE + dot(low, spread)

    live = jnp.where(
        lax.broadcasted_iota(jnp.int32, code.shape, 0) * span
        + lax.broadcasted_iota(jnp.int32, code.shape, 1)
        < atoms - padding_ref[0],
        code,
        0,
    ).astype(F32)
    for r in range(code.shape[0]):
        if any(
            r * span < row + rows and row < (r + 1) * span
            for side in sides
            for source, row, rows, _ in side.pieces
            if source == "act"
        ):
            code_ref[(r + 1) * span : (r + 2) * span, :] = column_of(live[r : r + 1], span)
    for copy in code_copies:
        copy.wait()
    if edge:
        for i, at in enumerate((0, atoms + span)):
            two = halo_code_ref[i].astype(F32)
            row = two[0:1, :] * CODE_BASE + two[1:2, :]
            code_ref[at : at + span, :] = column_of(row, span)

    w_kv = jnp.concatenate([wk_ref[...], wv_ref[...]], axis=1)
    w_qg = jnp.concatenate([wq_ref[...], wg_ref[...]], axis=1)
    for n, side in enumerate(sides):
        for s in range(samples):
            block = n * samples + s
            for copy in part_copies.get((n, s), []):
                copy.wait()
            kv = dot(act_ref[block], w_kv)
            k_refs[block][...] = kv[:, :channels]
            v_refs[block][...] = kv[:, channels:]
            dk_refs[block][...] = jnp.zeros_like(dk_refs[block])
            dv_refs[block][...] = jnp.zeros_like(dv_refs[block])
            at = side.query_row - side.origin
            qg = dot(act_ref[block, at : at + side.queries, :], w_qg)
            q_ref[block] = qg[:, :channels].astype(BF16)
            gate = jax.nn.sigmoid(qg[:, channels:])
            gy = dot_nt(gout_ref[block], wo_ref[...])
            g_ref[block] = gate
            gy_ref[block] = gy
            datt_ref[block] = (gy * gate).astype(BF16)

    for copy in pair_copies:
        copy.wait()

    def by_head(rows):
        return jnp.concatenate(
            [
                rows[half * half_rows : (half + 1) * half_rows] * head_masks_b[h]
                for half in range(2)
                for h in range(heads)
            ],
            axis=0,
        )

    def own_head(wide):
        halves = []
        for half in range(2):
            total = None
            for h in range(heads):
                at = (half * heads + h) * half_rows
                term = wide[at : at + half_rows] * head_masks[h]
                total = term if total is None else total + term
            halves.append(total)
        return jnp.concatenate(halves, axis=0)

    def window_group(members, w, tok_sum):
        keys, qrows, same, pair_w = [], [], [], []
        for lane_slot, (n, side, first, shift) in enumerate(members):
            window = side.first + shift + w
            start = jnp.clip(
                anchor + window * win_rows + offsets_ref[window], 0, all_atoms - span
            ) - (anchor + side.origin)
            start = jnp.clip(start, 0, side.rows - span)
            key_codes = code_ref[pl.ds(start + (side.origin + span), span), :]
            query_codes = qcode_ref[window % per_row, pl.ds(window // per_row, 1), :]
            same.append(key_codes == query_codes)
            pair_w.append(pair_ref.at[first + shift + w])
            bias = dot_tn(pair_w[-1][...], wexp_ref[...]) + jnp.where(same[-1], wtok, 0.0)
            bias_ref[lane_slot] = jnp.where(key_codes > 0.0, bias, MASKED) * LOG2E
            at = pl.multiple_of((shift + w) * win_rows, win_rows)
            qrows.append(pl.ds(at, win_rows))
            keys.append(pl.ds(start, span))

        def products(m, s):
            block = members[m][0] * samples + s
            kb = k_refs[block][keys[m], :].astype(BF16)
            vb = v_refs[block][keys[m], :].astype(BF16)
            qh = by_head(q_ref[block, qrows[m], :])
            dh = by_head(datt_ref[block, qrows[m], :])
            return kb, vb, qh, dh, dot_nt(kb, qh), dot_nt(vb, dh)

        def softmax(m, state):
            kb, vb, qh, dh, x, dp = state
            x = x * (scale * LOG2E) + bias_ref[m]
            e = jnp.exp2(x - jnp.max(x, axis=0, keepdims=True))
            p = e * (1.0 / jnp.sum(e, axis=0, keepdims=True))
            t = p * dp
            ds = t - p * jnp.sum(t, axis=0, keepdims=True)
            return kb, vb, qh, dh, p.astype(BF16), ds

        def gradients(m, s, state):
            block = members[m][0] * samples + s
            kb, vb, qh, dh, pb, ds = state
            dsb = ds.astype(BF16)
            if s == 0:
                bsum_ref[m] = ds
            else:
                bsum_ref[m] += ds
            dk_refs[block][keys[m], :] += dot(dsb, qh)
            dv_refs[block][keys[m], :] += dot(pb, dh)
            att = own_head(dot_tn(pb, vb))
            rows = qrows[m]
            dq_ref[block, rows, :] = (own_head(dot_tn(dsb, kb)) * scale).astype(BF16)
            gate = g_ref[block, rows, :]
            ga = gate * att
            gated_ref[block, rows, :] = ga.astype(BF16)
            dgate_ref[block, rows, :] = (gy_ref[block, rows, :] * ga * (1.0 - gate)).astype(BF16)

        order = [(m, s) for s in range(samples) for m in range(len(members))]
        states = [products(m, s) for m, s in order]
        states = [softmax(m, state) for (m, _), state in zip(order, states)]
        for (m, s), state in zip(order, states):
            gradients(m, s, state)
        width = heads * half_rows
        for m, (n, side, first, shift) in enumerate(members):
            total = bsum_ref[m]
            pw_ref[...] += dot(pair_w[m][...], total.astype(BF16))
            tok_sum += jnp.sum(jnp.where(same[m], total, 0.0), axis=0, keepdims=True)
            bsum_ref[m] = total.T
            slot = first + shift + w
            mine_ref[slot] = bsum_ref[m, pl.ds(pl.multiple_of(core * width, width), width), :]
            other_ref[slot] = bsum_ref[
                m, pl.ds(pl.multiple_of((1 - core) * width, width), width), :
            ].astype(BF16)
        return tok_sum

    tok_sum = jnp.zeros((1, lanes), F32)
    if len(sides) == 2:
        members = [(0, sides[0], 0, 0), (1, sides[1], sides[0].count, 0)]
        tok_sum = lax.fori_loop(
            0, sides[0].count, functools.partial(window_group, members), tok_sum
        )
    else:
        half = sides[0].count // 2
        members = [(0, sides[0], 0, 0), (0, sides[0], 0, half)]
        tok_sum = lax.fori_loop(0, half, functools.partial(window_group, members), tok_sum)
        if sides[0].count % 2:
            rest = [(0, sides[0], 0, sides[0].count - 1)]
            tok_sum = window_group(rest, 0, tok_sum)

    out_copies = []

    def send_out(source, target):
        out_copies.append(pltpu.make_async_copy(source, target, out_sem.at[len(out_copies)]))
        out_copies[-1].start()

    send_out(mine_ref, mine_hbm)
    send_out(other_ref, other_hbm)

    pending = []
    acc_kv = jnp.zeros((channels, 2 * channels), F32)
    acc_qg = jnp.zeros((channels, 2 * channels), F32)
    acc_o = jnp.zeros((channels, channels), F32)
    for n, side in enumerate(sides):
        at = side.query_row - side.origin
        for s in range(samples):
            block = n * samples + s
            dkv_b = jnp.concatenate(
                [(dk_refs[block][...] * scale).astype(BF16), dv_refs[block][...].astype(BF16)],
                axis=1,
            )
            dqg = jnp.concatenate([dq_ref[block], dgate_ref[block]], axis=1)
            part = dot_nt(dkv_b, w_kv)
            middle = part[at : at + side.queries] + dot_nt(dqg, w_qg)
            runs = [(0, part[:at]), (at, middle), (at + side.queries, part[at + side.queries :])]
            for run_at, run in runs:
                if run.shape[0] == 0:
                    continue
                run = run.astype(BF16)
                for source, _, rows, piece_at in side.pieces:
                    low = max(run_at, piece_at)
                    high = min(run_at + run.shape[0], piece_at + rows)
                    if low >= high:
                        continue
                    value = run[low - run_at : high - run_at]
                    if source == "lo":
                        ga_halo_ref[1 - odd, s, low - piece_at : high - piece_at, :] = value
                    elif source == "hi":
                        ga_halo_ref[odd, s, low - piece_at : high - piece_at, :] = value
                    else:
                        ga_refs[n][s, low - piece_at : high - piece_at, :] = value
            pending.append((dkv_b, dqg))
    if edge:
        for i, out_ref in enumerate(ga_out_refs):
            send_out(ga_halo_ref.at[i], out_ref)
    for ga_ref, out_ref in zip(ga_refs, ga_hbm):
        send_out(ga_ref, out_ref)
    for n, side in enumerate(sides):
        at = side.query_row - side.origin
        for s in range(samples):
            block = n * samples + s
            dkv_b, dqg = pending[block]
            acc_kv = acc_kv + dot_tn(act_ref[block], dkv_b)
            acc_qg = acc_qg + dot_tn(act_ref[block, at : at + side.queries, :], dqg)
            acc_o = acc_o + dot_tn(gated_ref[block], gout_ref[block])

    diag = lax.broadcasted_iota(jnp.int32, (win_rows * cp, lanes), 0) // cp == lane_row
    pw = jnp.where(diag, pw_ref[...], 0.0).reshape(win_rows, cp, lanes).sum(axis=0)
    parts = [
        acc_qg[:, :channels],
        acc_kv[:, :channels],
        acc_kv[:, channels:],
        acc_qg[:, channels:],
        acc_o,
    ]
    first_half, second_half = [], []
    left = out_half
    for part in parts:
        if left >= channels:
            first_half.append(part)
            left -= channels
        elif left > 0:
            first_half.append(part[:left])
            second_half.append(part[left:])
            left = 0
        else:
            second_half.append(part)
    tok_rows = jnp.where(
        lax.broadcasted_iota(jnp.int32, (SMALL_ROWS, lanes), 0) == 0, tok_sum, 0.0
    )
    for half, group in enumerate((first_half + [pw], second_half + [tok_rows])):
        at = 0
        for part in group:
            rows = part.shape[0]
            if chained:
                part = part + acc_in_ref[half, at : at + rows, :]
            acc_ref[half, at : at + rows, :] = part
            at += rows
    if last:
        acc_mine_ref[...] = acc_ref[core]
        value = acc_ref[1 - core]
        wide = value.shape[0] - SMALL_ROWS
        top = value.astype(BF16)
        acc_other_ref[: wide + SMALL_ROWS, :] = top
        rest = value[wide:] - top[wide:].astype(F32)
        acc_other_ref[wide + SMALL_ROWS :, :] = rest.astype(BF16)
    for copy in out_copies:
        copy.wait()


def pair_kernel(wpair_ref, *refs, order, heads, cp):
    out_ref = refs[-1]
    rows = refs[0].shape[1]
    half_rows = rows // heads
    lane = lax.broadcasted_iota(jnp.int32, (1, rows), 1)
    pick = (
        lax.broadcasted_iota(jnp.int32, (heads, rows), 0)
        == lax.broadcasted_iota(jnp.int32, (heads, rows), 1) // half_rows
    ).astype(BF16)
    wlane = dot_tn(wpair_ref[...], pick)
    wexp = jnp.concatenate(
        [jnp.where(lane % half_rows == i, wlane, 0.0) for i in range(half_rows)], axis=0
    ).astype(BF16)
    for which, group in enumerate(order):
        m_ref, r_ref = refs[2 * which], refs[2 * which + 1]
        for slot, window in enumerate(group):
            total = (m_ref[slot] + r_ref[slot].astype(F32)).astype(BF16)
            out_ref[window] = dot(wexp, total).astype(BF16)


def act_sum_kernel(firsts, *refs):
    out_ref = refs[-1]
    atoms = out_ref.shape[1]
    is_odd = lax.axis_index("atoms") % 2 == 1
    from_a, from_b = refs[-3][...].astype(F32), refs[-2][...].astype(F32)
    halos = [jnp.where(is_odd, from_a, from_b), jnp.where(is_odd, from_b, from_a)]
    span = from_a.shape[1]
    halo_rows = [(0, halos[0]), (atoms - span, halos[1])]
    marks = {0, span, atoms - span, atoms}
    for first, ref in zip(firsts, refs):
        marks |= {first, first + ref.shape[1]}
    marks = sorted(marks)
    for low, high in zip(marks[:-1], marks[1:]):
        total = None
        for first, halo in halo_rows:
            if first <= low and high <= first + span:
                total = halo[:, low - first : high - first]
        for first, ref in zip(firsts, refs):
            if first <= low and high <= first + ref.shape[1]:
                term = ref[:, low - first : high - first, :].astype(F32)
                total = term if total is None else total + term
        out_ref[:, low:high, :] = total.astype(BF16)


def finish_kernel(sent_ref, got_ref, gw_ref, gpw_ref, gtok_ref, *, heads):
    rows = sent_ref.shape[0]
    wide = rows - 2 * SMALL_ROWS
    channels = gw_ref.shape[1]
    is_first = lax.axis_index("samples") == 0
    sent, got = sent_ref[...].astype(F32), got_ref[...].astype(F32)
    first = jnp.where(is_first, sent, got)
    second = jnp.where(is_first, got, sent)
    gw_ref[:wide, :] = first[:wide]
    gw_ref[wide:, :] = second[:wide]
    pw = first[wide : wide + SMALL_ROWS] + first[wide + SMALL_ROWS :]
    tok = second[wide : wide + 1] + second[wide + SMALL_ROWS : wide + SMALL_ROWS + 1]
    half_rows = channels // (2 * heads)
    head = (lax.broadcasted_iota(jnp.int32, (heads, channels), 1) // half_rows) % heads
    pick = (head == lax.broadcasted_iota(jnp.int32, (heads, channels), 0)).astype(F32)
    gpw_ref[...] = lax.dot_general(
        pick,
        pw,
        (((1,), (1,)), ((), ())),
        precision=lax.Precision.HIGHEST,
        preferred_element_type=F32,
    )
    for h in range(heads):
        gtok_ref[h] = jnp.sum(tok * pick[h : h + 1])


def per_device(
    act,
    grad_out,
    pair,
    w_query,
    w_key,
    w_value,
    w_gate,
    w_out,
    w_pair,
    w_token,
    offsets,
    atom_token,
    padding,
):
    samples, atoms, channels = act.shape
    windows = offsets.shape[0]
    win_rows = atoms // windows
    span = pair.shape[-1]
    cp, heads = w_pair.shape
    half_rows = win_rows // 2
    lanes = heads * win_rows
    ranges = lax.axis_size("atoms")
    cores = lax.axis_size("samples")
    assert cores == 2 and ranges & (ranges - 1) == 0
    tok = atom_token.reshape(atoms // span, span)
    w_pair_t = w_pair.T
    vmem = pl.BlockSpec(memory_space=pltpu.VMEM)
    smem = pl.BlockSpec(memory_space=pltpu.SMEM)
    hbm = pl.BlockSpec(memory_space=pl.ANY)

    exchanges = [
        [pair for i in range(first, ranges - 1, 2) for pair in ((i, i + 1), (i + 1, i))]
        for first in range(2)
    ]
    last_block = atoms // span - 1
    to_send = pl.pallas_call(
        payload_kernel,
        out_shape=[jax.ShapeDtypeStruct((samples + 1, span, channels), BF16)] * 2,
        grid=(1,),
        in_specs=[
            pl.BlockSpec((samples, span, channels), lambda i: (0, last_block, 0)),
            pl.BlockSpec((samples, span, channels), lambda i: (0, 0, 0)),
            vmem,
            smem,
        ],
        out_specs=[vmem, vmem],
    )(act, act, tok, padding)
    halos = [lax.ppermute(part, "atoms", swaps) for part, swaps in zip(to_send, exchanges)]

    out_half = 5 * channels // 2
    part_rows = out_half + SMALL_ROWS
    coded_rows = part_rows + SMALL_ROWS
    geo = (samples, atoms, channels, heads, win_rows, span, cp, out_half)
    pair_flat = pair.reshape(windows, win_rows * cp, span)
    width = heads * half_rows
    common = (
        offsets,
        padding,
        w_token,
        tok,
        act,
        grad_out,
        pair_flat,
        w_query,
        w_key,
        w_value,
        w_gate,
        w_out,
        w_pair_t,
    )
    shape = jax.ShapeDtypeStruct

    def call(sides, halos=(), acc_in=None, last=False):
        edge, chained = len(halos) > 0, acc_in is not None
        args = common + tuple(halos) + ((acc_in,) if chained else ())
        in_specs = [smem] * 3 + [vmem] + [hbm] * 3 + [vmem] * 6 + [hbm] * len(halos)
        in_specs += [vmem] * chained
        count = sum(side.count for side in sides)
        queries, rows = sides[0].queries, sides[0].rows
        blocks = len(sides) * samples
        own_rows = [sum(p[2] for p in side.pieces if p[0] == "act") for side in sides]
        out_shape = [shape((samples, n, channels), BF16) for n in own_rows]
        if edge:
            out_shape += [shape((samples, span, channels), BF16)] * 2
        if last:
            out_shape += [shape((part_rows, channels), F32), shape((coded_rows, channels), BF16)]
        else:
            out_shape += [shape((2, part_rows, channels), F32)]
        out_specs = [hbm] * (len(own_rows) + 2 * edge) + [vmem] * (1 + last) + [hbm] * 2
        out_shape += [shape((count, width, span), F32), shape((count, width, span), BF16)]
        per_query = (blocks, queries, channels)
        scratch = [
            pltpu.VMEM((count, win_rows * cp, span), BF16),
            pltpu.SemaphoreType.DMA((len(sides) + 2,)),
            pltpu.VMEM((win_rows * cp, lanes), BF16),
            pltpu.VMEM((win_rows * cp, lanes), F32),
            pltpu.VMEM((atoms + 2 * span, span), F32),
            pltpu.VMEM((span // win_rows, -(-atoms // span // 8) * 8, lanes), F32),
            pltpu.VMEM((2, CODE_ROWS, span), BF16),
            pltpu.VMEM((blocks, rows, channels), BF16),
            pltpu.VMEM(per_query, BF16),
            pltpu.SemaphoreType.DMA((len(sides), 2, 3)),
            pltpu.VMEM(per_query, BF16),
            pltpu.VMEM(per_query, BF16),
            pltpu.VMEM(per_query, F32),
            pltpu.VMEM(per_query, F32),
            pltpu.VMEM(per_query, BF16),
            pltpu.VMEM(per_query, BF16),
            pltpu.VMEM(per_query, BF16),
            pltpu.VMEM((2, span, lanes), F32),
            pltpu.VMEM((2, span, lanes), F32),
        ]
        if last:
            scratch += [pltpu.VMEM((2, part_rows, channels), F32)]
        if edge:
            scratch += [
                pltpu.VMEM((2, samples, span, channels), BF16),
            ]
        scratch += [pltpu.VMEM((samples, n, channels), BF16) for n in own_rows]
        scratch += [
            pltpu.VMEM((count, width, span), F32),
            pltpu.VMEM((count, width, span), BF16),
            pltpu.SemaphoreType.DMA((len(sides) + 2 + 2 * edge,)),
        ]
        scratch += [pltpu.VMEM((rows, channels), F32)] * (4 * blocks)
        units = 6 * count * samples + 8 * count + 14 * blocks
        return pl.pallas_call(
            functools.partial(attention_kernel, geo, sides, edge, chained, last),
            out_shape=out_shape,
            in_specs=in_specs,
            out_specs=out_specs,
            scratch_shapes=scratch,
            compiler_params=pltpu.CompilerParams(vmem_limit_bytes=VMEM_LIMIT),
            cost_estimate=pl.CostEstimate(
                flops=2 * units * 128 * 128 * 128 * 4,
                bytes_accessed=12_000_000,
                transcendentals=count * samples * span * lanes,
            ),
        )(*args)

    edge_count = span // win_rows
    early_count = (windows - 2 * edge_count) * EARLY_SHARE // 12
    early = tuple(range(edge_count, edge_count + early_count))
    late = tuple(range(edge_count + early_count, windows - edge_count))
    low, high = tuple(range(edge_count)), tuple(range(windows - edge_count, windows))
    early_end = (early[-1] + 1) * win_rows + span
    late_first = late[0] * win_rows - span
    own = edge_count * win_rows + span
    swap = [(0, 1), (1, 0)]

    early_side = Side(early, win_rows, early_end, [("act", 0, early_end, 0)], 0)
    ga_early, acc, mine1, other1 = call([early_side])
    recv1 = lax.ppermute(other1, "samples", swap)

    low_side = Side(low, win_rows, own + span, [("lo", 0, span, 0), ("act", 0, own, span)], -span)
    high_side = Side(
        high,
        win_rows,
        own + span,
        [("act", atoms - own, own, 0), ("hi", 0, span, own)],
        atoms - own,
    )
    ga_low, ga_high, ga_a, ga_b, acc, mine2, other2 = call([low_side, high_side], halos, acc)
    recv2 = lax.ppermute(other2, "samples", swap)
    from_a, from_b = [
        lax.ppermute(part, "atoms", swaps) for part, swaps in zip((ga_a, ga_b), exchanges)
    ]

    late_rows = atoms - late_first
    late_side = Side(
        late, win_rows, late_rows, [("act", late_first, late_rows, 0)], late_first
    )
    ga_late, acc_mine, acc_other, mine3, other3 = call([late_side], (), acc, True)

    wide = out_half

    def encode(value):
        top = lax.reduce_precision(value, 8, 7)
        return jnp.concatenate([top, value[wide:] - top[wide:]]).astype(BF16)

    def decode(sent):
        sent = sent.astype(F32)
        return jnp.concatenate(
            [sent[:wide], sent[wide : wide + SMALL_ROWS] + sent[wide + SMALL_ROWS :]]
        )

    acc_other, other3, from_a, from_b = lax.optimization_barrier(
        (acc_other, other3, from_a, from_b)
    )
    recv3 = lax.ppermute(other3, "samples", swap)
    total = acc_mine + decode(lax.ppermute(acc_other, "samples", swap))
    def sum_pair(mine3):
        return pl.pallas_call(
            functools.partial(pair_kernel, order=(early, low + high, late), heads=heads, cp=cp),
            out_shape=shape((windows, half_rows * cp, span), BF16),
            in_specs=[vmem] * 7,
            out_specs=vmem,
            compiler_params=pltpu.CompilerParams(vmem_limit_bytes=VMEM_LIMIT),
            cost_estimate=pl.CostEstimate(
                flops=2 * windows * 256 * 256 * 256, bytes_accessed=4_000_000, transcendentals=0
            ),
        )(w_pair_t, mine1, recv1, mine2, recv2, mine3, recv3)

    def sum_act(ga_late):
        pieces = [
            (0, ga_early),
            (late_first, ga_late),
            (0, ga_low),
            (atoms - own, ga_high),
        ]
        parts = [part for _, part in pieces] + [from_a, from_b]
        return pl.pallas_call(
            functools.partial(act_sum_kernel, [first for first, _ in pieces]),
            out_shape=shape((samples, atoms, channels), BF16),
            grid=(2,),
            in_specs=[
                pl.BlockSpec((samples // 2,) + part.shape[1:], lambda s: (s, 0, 0))
                for part in parts
            ],
            out_specs=pl.BlockSpec((samples // 2, atoms, channels), lambda s: (s, 0, 0)),
            compiler_params=pltpu.CompilerParams(vmem_limit_bytes=VMEM_LIMIT),
            cost_estimate=pl.CostEstimate(
                flops=4 * samples * atoms * channels, bytes_accessed=6_000_000, transcendentals=0
            ),
        )(*parts)

    step = ranges // 2
    grad_pair = grad_act = None
    while step >= 1:
        sent = encode(total)
        if grad_pair is None:
            sent, mine3 = lax.optimization_barrier((sent, mine3))
            grad_pair = sum_pair(mine3)
        elif grad_act is None:
            sent, ga_late = lax.optimization_barrier((sent, ga_late))
            grad_act = sum_act(ga_late)
        got = lax.ppermute(sent, "atoms", [(i, i ^ step) for i in range(ranges)])
        total = decode(sent) + decode(got)
        if step == ranges // 2:
            total, grad_pair = lax.optimization_barrier((total, grad_pair))
        elif step == ranges // 4:
            total, grad_act = lax.optimization_barrier((total, grad_act))
        step //= 2
    if grad_pair is None:
        grad_pair = sum_pair(mine3)
    if grad_act is None:
        grad_act = sum_act(ga_late)
    sent = encode(total)
    got = lax.ppermute(sent, "samples", swap)
    grad_weights, grad_pair_weight, grad_token_weight = pl.pallas_call(
        functools.partial(finish_kernel, heads=heads),
        out_shape=[
            shape((5 * channels, channels), F32),
            shape((heads, cp), F32),
            shape((heads,), F32),
        ],
        in_specs=[vmem, vmem],
        out_specs=[vmem, vmem, smem],
    )(sent, got)

    return (
        grad_act,
        grad_pair.reshape(windows, half_rows, cp, span),
        grad_weights.reshape(5, channels, channels),
        grad_pair_weight.T,
        grad_token_weight,
    )


def solution(mesh):
    in_specs = (
        P("samples", ("groups", "atoms"), None),
        P("samples", ("groups", "atoms"), None),
        P(("groups", "atoms"), None, None, None),
        P(),
        P(),
        P(),
        P(),
        P(),
        P(),
        P(),
        P(("groups", "atoms")),
        P(("groups", "atoms")),
        P(("groups", "atoms")),
    )
    out_specs = (
        P("samples", ("groups", "atoms"), None),
        P(("groups", "atoms"), "samples", None, None),
        P("groups", None, None),
        P("groups", None),
        P("groups"),
    )
    return jax.shard_map(
        per_device, mesh=mesh, in_specs=in_specs, out_specs=out_specs, check_vma=False
    )
```

```python
import functools
import math

import jax
import jax.numpy as jnp
from jax import lax
from jax.experimental import pallas as pl
from jax.experimental.pallas import tpu as pltpu
from jax.sharding import PartitionSpec as P

BF16 = jnp.bfloat16
F32 = jnp.float32
MASKED = -1000000000.0
LOG2E = math.log2(math.e)
CODE_ROWS = 16
CODE_BASE = 128
SMALL_ROWS = 16
VMEM_LIMIT = 62 * 1024 * 1024
EARLY_SHARE = 6


def dot(a, b):
    return lax.dot_general(a, b, (((1,), (0,)), ((), ())), preferred_element_type=F32)


def dot_nt(a, b):
    return lax.dot_general(a, b, (((1,), (1,)), ((), ())), preferred_element_type=F32)


def dot_tn(a, b):
    return lax.dot_general(a, b, (((0,), (0,)), ((), ())), preferred_element_type=F32)


def column_of(row, span):
    return jnp.broadcast_to(row, (span, row.shape[-1])).T


class Side:
    def __init__(self, windows, win_rows, rows, pieces, origin):
        self.first = windows[0]
        self.count = len(windows)
        self.queries = len(windows) * win_rows
        self.query_row = windows[0] * win_rows
        self.rows = rows
        self.pieces = pieces
        self.origin = origin


class HaloCopy:
    def __init__(self, is_odd, when_odd, when_even, target, sem):
        self.is_odd = is_odd
        self.options = [pltpu.make_async_copy(s, target, sem) for s in (when_even, when_odd)]

    def start(self):
        pl.when(self.is_odd)(self.options[1].start)
        pl.when(jnp.logical_not(self.is_odd))(self.options[0].start)

    def wait(self):
        self.options[0].wait()


def payload_kernel(high_ref, low_ref, tok_ref, padding_ref, out_a_ref, out_b_ref):
    samples, span, _ = high_ref.shape
    rows = tok_ref.shape[0]
    atoms = rows * span
    index = lax.broadcasted_iota(jnp.int32, (span, span), 0)
    place = lax.broadcasted_iota(jnp.int32, (1, span), 1)

    def write(out_ref, act_ref, row):
        out_ref[:samples] = act_ref[...]
        live = place + row * span < atoms - padding_ref[0]
        code = jnp.where(live, tok_ref[row : row + 1, :] + 1, 0)
        top, low = code // CODE_BASE, code % CODE_BASE
        both = jnp.where(index == 0, top, jnp.where(index == 1, low, 0))
        out_ref[samples] = both.astype(F32).astype(BF16)

    is_odd = lax.axis_index("atoms") % 2 == 1

    @pl.when(is_odd)
    def _():
        write(out_a_ref, low_ref, 0)
        write(out_b_ref, high_ref, rows - 1)

    @pl.when(jnp.logical_not(is_odd))
    def _():
        write(out_a_ref, high_ref, rows - 1)
        write(out_b_ref, low_ref, 0)


def attention_kernel(geo, sides, edge, chained, last, *refs):
    samples, atoms, channels, heads, win_rows, span, cp, out_half = geo
    refs = list(refs)
    take = lambda n: [refs.pop(0) for _ in range(n)]
    offsets_ref, padding_ref, wtok_ref = take(3)
    tok_ref, act_hbm, gout_hbm, pair_hbm = take(4)
    wq_ref, wk_ref, wv_ref, wg_ref, wo_ref, wpair_ref = take(6)
    if edge:
        halo_a, halo_b = take(2)
    if chained:
        (acc_in_ref,) = take(1)
    ga_hbm = take(len(sides))
    if edge:
        ga_out_refs = take(2)
    if last:
        acc_mine_ref, acc_other_ref = take(2)
    else:
        (acc_ref,) = take(1)
    mine_hbm, other_hbm = take(2)
    pair_ref, pair_sem, wexp_ref, pw_ref, code_ref, qcode_ref, halo_code_ref = take(7)
    act_ref, gout_ref, in_sem, q_ref, datt_ref, g_ref, gy_ref = take(7)
    dq_ref, dgate_ref, gated_ref, bias_ref, bsum_ref = take(5)
    if last:
        (acc_ref,) = take(1)
    if edge:
        (ga_halo_ref,) = take(1)
    ga_refs = take(len(sides))
    mine_ref, other_ref, out_sem = take(3)
    n_blocks = len(sides) * samples
    k_refs = take(n_blocks)
    v_refs = take(n_blocks)
    dk_refs = take(n_blocks)
    dv_refs = take(n_blocks)

    half_rows = win_rows // 2
    head_dim = channels // heads
    scale = 1.0 / math.sqrt(head_dim)
    rank = lax.axis_index("atoms")
    core = lax.axis_index("samples")
    anchor = rank * atoms
    all_atoms = lax.axis_size("atoms") * atoms
    odd = rank % 2
    is_odd = odd == 1

    def halo_copy(source, place, target, sem):
        refs = (halo_a, halo_b) if source == "lo" else (halo_b, halo_a)
        return HaloCopy(is_odd, *[ref.at[place] for ref in refs], target, sem)


    part = samples // 4
    part_copies = {}
    for n, side in enumerate(sides):
        for s in range(0, samples, part):
            run = pl.ds(s, part)
            block_run = pl.ds(n * samples + s, part)
            mine = []
            for i, (source, row, rows, at) in enumerate(side.pieces):
                target, sem = act_ref.at[block_run, pl.ds(at, rows)], in_sem.at[n, s // part, i]
                if source == "act":
                    mine.append(
                        pltpu.make_async_copy(act_hbm.at[run, pl.ds(row, rows)], target, sem)
                    )
                else:
                    mine.append(halo_copy(source, run, target, sem))
            mine.append(
                pltpu.make_async_copy(
                    gout_hbm.at[run, pl.ds(side.query_row, side.queries)],
                    gout_ref.at[block_run],
                    in_sem.at[n, s // part, 2],
                )
            )
            part_copies[n, s] = mine
    code_copies = []
    if edge:
        for i, source in enumerate(("lo", "hi")):
            code_copies.append(
                halo_copy(
                    source,
                    (samples, pl.ds(0, CODE_ROWS)),
                    halo_code_ref.at[i],
                    pair_sem.at[len(sides) + i],
                )
            )
    pair_copies = []
    first = 0
    for n, side in enumerate(sides):
        pair_copies.append(
            pltpu.make_async_copy(
                pair_hbm.at[pl.ds(side.first, side.count)],
                pair_ref.at[pl.ds(first, side.count)],
                pair_sem.at[n],
            )
        )
        first += side.count
    for copy in code_copies:
        copy.start()
    for copies in part_copies.values():
        for copy in copies:
            copy.start()
    for copy in pair_copies:
        copy.start()

    lane = lax.broadcasted_iota(jnp.int32, (1, channels), 1)
    head_masks = [(lane // head_dim == h).astype(F32) for h in range(heads)]
    head_masks_b = [m.astype(BF16) for m in head_masks]

    lanes = 2 * heads * half_rows
    s_lane = lax.broadcasted_iota(jnp.int32, (1, lanes), 1)
    lane_head = (s_lane // half_rows) % heads
    lane_row = (s_lane // (heads * half_rows)) * half_rows + s_lane % half_rows
    wtok = jnp.zeros((1, lanes), F32)
    for h in range(heads):
        wtok = jnp.where(lane_head == h, wtok_ref[h], wtok)
    pick = (
        lax.broadcasted_iota(jnp.int32, (heads, lanes), 0)
        == (lax.broadcasted_iota(jnp.int32, (heads, lanes), 1) // half_rows) % heads
    ).astype(BF16)
    wlane = dot_tn(wpair_ref[...], pick).astype(BF16)
    for i in range(win_rows):
        wexp_ref[i * cp : (i + 1) * cp, :] = jnp.where(lane_row == i, wlane, 0.0).astype(BF16)
    pw_ref[...] = jnp.zeros_like(pw_ref)

    per_row = span // win_rows
    code = tok_ref[...] + 1
    top = (code // CODE_BASE).astype(F32).astype(BF16)
    low = (code % CODE_BASE).astype(F32).astype(BF16)
    source_lane = lax.broadcasted_iota(jnp.int32, (span, lanes), 0)
    for m in range(per_row):
        spread = (source_lane == m * win_rows + lane_row).astype(F32).astype(BF16)
        qcode_ref[m, : code.shape[0], :] = dot(top, spread) * CODE_BASE + dot(low, spread)

    live = jnp.where(
        lax.broadcasted_iota(jnp.int32, code.shape, 0) * span
        + lax.broadcasted_iota(jnp.int32, code.shape, 1)
        < atoms - padding_ref[0],
        code,
        0,
    ).astype(F32)
    for r in range(code.shape[0]):
        if any(
            r * span < row + rows and row < (r + 1) * span
            for side in sides
            for source, row, rows, _ in side.pieces
            if source == "act"
        ):
            code_ref[(r + 1) * span : (r + 2) * span, :] = column_of(live[r : r + 1], span)
    for copy in code_copies:
        copy.wait()
    if edge:
        for i, at in enumerate((0, atoms + span)):
            two = halo_code_ref[i].astype(F32)
            row = two[0:1, :] * CODE_BASE + two[1:2, :]
            code_ref[at : at + span, :] = column_of(row, span)

    w_kv = jnp.concatenate([wk_ref[...], wv_ref[...]], axis=1)
    w_qg = jnp.concatenate([wq_ref[...], wg_ref[...]], axis=1)
    for n, side in enumerate(sides):
        for s in range(samples):
            block = n * samples + s
            for copy in part_copies.get((n, s), []):
                copy.wait()
            kv = dot(act_ref[block], w_kv)
            k_refs[block][...] = kv[:, :channels]
            v_refs[block][...] = kv[:, channels:]
            dk_refs[block][...] = jnp.zeros_like(dk_refs[block])
            dv_refs[block][...] = jnp.zeros_like(dv_refs[block])
            at = side.query_row - side.origin
            qg = dot(act_ref[block, at : at + side.queries, :], w_qg)
            q_ref[block] = qg[:, :channels].astype(BF16)
            gate = jax.nn.sigmoid(qg[:, channels:])
            gy = dot_nt(gout_ref[block], wo_ref[...])
            g_ref[block] = gate
            gy_ref[block] = gy
            datt_ref[block] = (gy * gate).astype(BF16)

    for copy in pair_copies:
        copy.wait()

    def by_head(rows):
        return jnp.concatenate(
            [
                rows[half * half_rows : (half + 1) * half_rows] * head_masks_b[h]
                for half in range(2)
                for h in range(heads)
            ],
            axis=0,
        )

    def own_head(wide):
        halves = []
        for half in range(2):
            total = None
            for h in range(heads):
                at = (half * heads + h) * half_rows
                term = wide[at : at + half_rows] * head_masks[h]
                total = term if total is None else total + term
            halves.append(total)
        return jnp.concatenate(halves, axis=0)

    def window_group(members, w, tok_sum):
        keys, qrows, same, pair_w = [], [], [], []
        for lane_slot, (n, side, first, shift) in enumerate(members):
            window = side.first + shift + w
            start = jnp.clip(
                anchor + window * win_rows + offsets_ref[window], 0, all_atoms - span
            ) - (anchor + side.origin)
            start = jnp.clip(start, 0, side.rows - span)
            key_codes = code_ref[pl.ds(start + (side.origin + span), span), :]
            query_codes = qcode_ref[window % per_row, pl.ds(window // per_row, 1), :]
            same.append(key_codes == query_codes)
            pair_w.append(pair_ref.at[first + shift + w])
            bias = dot_tn(pair_w[-1][...], wexp_ref[...]) + jnp.where(same[-1], wtok, 0.0)
            bias_ref[lane_slot] = jnp.where(key_codes > 0.0, bias, MASKED) * LOG2E
            at = pl.multiple_of((shift + w) * win_rows, win_rows)
            qrows.append(pl.ds(at, win_rows))
            keys.append(pl.ds(start, span))

        def products(m, s):
            block = members[m][0] * samples + s
            kb = k_refs[block][keys[m], :].astype(BF16)
            vb = v_refs[block][keys[m], :].astype(BF16)
            qh = by_head(q_ref[block, qrows[m], :])
            dh = by_head(datt_ref[block, qrows[m], :])
            return kb, vb, qh, dh, dot_nt(kb, qh), dot_nt(vb, dh)

        def softmax(m, state):
            kb, vb, qh, dh, x, dp = state
            x = x * (scale * LOG2E) + bias_ref[m]
            e = jnp.exp2(x - jnp.max(x, axis=0, keepdims=True))
            p = e * (1.0 / jnp.sum(e, axis=0, keepdims=True))
            t = p * dp
            ds = t - p * jnp.sum(t, axis=0, keepdims=True)
            return kb, vb, qh, dh, p.astype(BF16), ds

        def gradients(m, s, state):
            block = members[m][0] * samples + s
            kb, vb, qh, dh, pb, ds = state
            dsb = ds.astype(BF16)
            if s == 0:
                bsum_ref[m] = ds
            else:
                bsum_ref[m] += ds
            dk_refs[block][keys[m], :] += dot(dsb, qh)
            dv_refs[block][keys[m], :] += dot(pb, dh)
            att = own_head(dot_tn(pb, vb))
            rows = qrows[m]
            dq_ref[block, rows, :] = (own_head(dot_tn(dsb, kb)) * scale).astype(BF16)
            gate = g_ref[block, rows, :]
            ga = gate * att
            gated_ref[block, rows, :] = ga.astype(BF16)
            dgate_ref[block, rows, :] = (gy_ref[block, rows, :] * ga * (1.0 - gate)).astype(BF16)

        order = [(m, s) for s in range(samples) for m in range(len(members))]
        states = [products(m, s) for m, s in order]
        states = [softmax(m, state) for (m, _), state in zip(order, states)]
        for (m, s), state in zip(order, states):
            gradients(m, s, state)
        width = heads * half_rows
        for m, (n, side, first, shift) in enumerate(members):
            total = bsum_ref[m]
            pw_ref[...] += dot(pair_w[m][...], total.astype(BF16))
            tok_sum += jnp.sum(jnp.where(same[m], total, 0.0), axis=0, keepdims=True)
            bsum_ref[m] = total.T
            slot = first + shift + w
            mine_ref[slot] = bsum_ref[m, pl.ds(pl.multiple_of(core * width, width), width), :]
            other_ref[slot] = bsum_ref[
                m, pl.ds(pl.multiple_of((1 - core) * width, width), width), :
            ].astype(BF16)
        return tok_sum

    tok_sum = jnp.zeros((1, lanes), F32)
    if len(sides) == 2:
        members = [(0, sides[0], 0, 0), (1, sides[1], sides[0].count, 0)]
        tok_sum = lax.fori_loop(
            0, sides[0].count, functools.partial(window_group, members), tok_sum
        )
    else:
        half = sides[0].count // 2
        members = [(0, sides[0], 0, 0), (0, sides[0], 0, half)]
        tok_sum = lax.fori_loop(0, half, functools.partial(window_group, members), tok_sum)
        if sides[0].count % 2:
            rest = [(0, sides[0], 0, sides[0].count - 1)]
            tok_sum = window_group(rest, 0, tok_sum)

    out_copies = []

    def send_out(source, target):
        out_copies.append(pltpu.make_async_copy(source, target, out_sem.at[len(out_copies)]))
        out_copies[-1].start()

    send_out(mine_ref, mine_hbm)
    send_out(other_ref, other_hbm)

    pending = []
    acc_kv = jnp.zeros((channels, 2 * channels), F32)
    acc_qg = jnp.zeros((channels, 2 * channels), F32)
    acc_o = jnp.zeros((channels, channels), F32)
    for n, side in enumerate(sides):
        at = side.query_row - side.origin
        for s in range(samples):
            block = n * samples + s
            dkv_b = jnp.concatenate(
                [(dk_refs[block][...] * scale).astype(BF16), dv_refs[block][...].astype(BF16)],
                axis=1,
            )
            dqg = jnp.concatenate([dq_ref[block], dgate_ref[block]], axis=1)
            part = dot_nt(dkv_b, w_kv)
            middle = part[at : at + side.queries] + dot_nt(dqg, w_qg)
            runs = [(0, part[:at]), (at, middle), (at + side.queries, part[at + side.queries :])]
            for run_at, run in runs:
                if run.shape[0] == 0:
                    continue
                run = run.astype(BF16)
                for source, _, rows, piece_at in side.pieces:
                    low = max(run_at, piece_at)
                    high = min(run_at + run.shape[0], piece_at + rows)
                    if low >= high:
                        continue
                    value = run[low - run_at : high - run_at]
                    if source == "lo":
                        ga_halo_ref[1 - odd, s, low - piece_at : high - piece_at, :] = value
                    elif source == "hi":
                        ga_halo_ref[odd, s, low - piece_at : high - piece_at, :] = value
                    else:
                        ga_refs[n][s, low - piece_at : high - piece_at, :] = value
            pending.append((dkv_b, dqg))
    if edge:
        for i, out_ref in enumerate(ga_out_refs):
            send_out(ga_halo_ref.at[i], out_ref)
    for ga_ref, out_ref in zip(ga_refs, ga_hbm):
        send_out(ga_ref, out_ref)
    for n, side in enumerate(sides):
        at = side.query_row - side.origin
        for s in range(samples):
            block = n * samples + s
            dkv_b, dqg = pending[block]
            acc_kv = acc_kv + dot_tn(act_ref[block], dkv_b)
            acc_qg = acc_qg + dot_tn(act_ref[block, at : at + side.queries, :], dqg)
            acc_o = acc_o + dot_tn(gated_ref[block], gout_ref[block])

    diag = lax.broadcasted_iota(jnp.int32, (win_rows * cp, lanes), 0) // cp == lane_row
    pw = jnp.where(diag, pw_ref[...], 0.0).reshape(win_rows, cp, lanes).sum(axis=0)
    parts = [
        acc_qg[:, :channels],
        acc_kv[:, :channels],
        acc_kv[:, channels:],
        acc_qg[:, channels:],
        acc_o,
    ]
    first_half, second_half = [], []
    left = out_half
    for part in parts:
        if left >= channels:
            first_half.append(part)
            left -= channels
        elif left > 0:
            first_half.append(part[:left])
            second_half.append(part[left:])
            left = 0
        else:
            second_half.append(part)
    tok_rows = jnp.where(
        lax.broadcasted_iota(jnp.int32, (SMALL_ROWS, lanes), 0) == 0, tok_sum, 0.0
    )
    for half, group in enumerate((first_half + [pw], second_half + [tok_rows])):
        at = 0
        for part in group:
            rows = part.shape[0]
            if chained:
                part = part + acc_in_ref[half, at : at + rows, :]
            acc_ref[half, at : at + rows, :] = part
            at += rows
    if last:
        acc_mine_ref[...] = acc_ref[core]
        value = acc_ref[1 - core]
        wide = value.shape[0] - SMALL_ROWS
        top = value.astype(BF16)
        acc_other_ref[: wide + SMALL_ROWS, :] = top
        rest = value[wide:] - top[wide:].astype(F32)
        acc_other_ref[wide + SMALL_ROWS :, :] = rest.astype(BF16)
    for copy in out_copies:
        copy.wait()


def pair_kernel(wpair_ref, *refs, order, heads, cp):
    out_ref = refs[-1]
    rows = refs[0].shape[1]
    half_rows = rows // heads
    lane = lax.broadcasted_iota(jnp.int32, (1, rows), 1)
    pick = (
        lax.broadcasted_iota(jnp.int32, (heads, rows), 0)
        == lax.broadcasted_iota(jnp.int32, (heads, rows), 1) // half_rows
    ).astype(BF16)
    wlane = dot_tn(wpair_ref[...], pick)
    wexp = jnp.concatenate(
        [jnp.where(lane % half_rows == i, wlane, 0.0) for i in range(half_rows)], axis=0
    ).astype(BF16)
    for which, group in enumerate(order):
        m_ref, r_ref = refs[2 * which], refs[2 * which + 1]
        for slot, window in enumerate(group):
            total = (m_ref[slot] + r_ref[slot].astype(F32)).astype(BF16)
            out_ref[window] = dot(wexp, total).astype(BF16)


def act_sum_kernel(firsts, *refs):
    out_ref = refs[-1]
    atoms = out_ref.shape[1]
    is_odd = lax.axis_index("atoms") % 2 == 1
    from_a, from_b = refs[-3][...].astype(F32), refs[-2][...].astype(F32)
    halos = [jnp.where(is_odd, from_a, from_b), jnp.where(is_odd, from_b, from_a)]
    span = from_a.shape[1]
    halo_rows = [(0, halos[0]), (atoms - span, halos[1])]
    marks = {0, span, atoms - span, atoms}
    for first, ref in zip(firsts, refs):
        marks |= {first, first + ref.shape[1]}
    marks = sorted(marks)
    for low, high in zip(marks[:-1], marks[1:]):
        total = None
        for first, halo in halo_rows:
            if first <= low and high <= first + span:
                total = halo[:, low - first : high - first]
        for first, ref in zip(firsts, refs):
            if first <= low and high <= first + ref.shape[1]:
                term = ref[:, low - first : high - first, :].astype(F32)
                total = term if total is None else total + term
        out_ref[:, low:high, :] = total.astype(BF16)


def finish_kernel(sent_ref, got_ref, gw_ref, gpw_ref, gtok_ref, *, heads):
    rows = sent_ref.shape[0]
    wide = rows - 2 * SMALL_ROWS
    channels = gw_ref.shape[1]
    is_first = lax.axis_index("samples") == 0
    sent, got = sent_ref[...].astype(F32), got_ref[...].astype(F32)
    first = jnp.where(is_first, sent, got)
    second = jnp.where(is_first, got, sent)
    gw_ref[:wide, :] = first[:wide]
    gw_ref[wide:, :] = second[:wide]
    pw = first[wide : wide + SMALL_ROWS] + first[wide + SMALL_ROWS :]
    tok = second[wide : wide + 1] + second[wide + SMALL_ROWS : wide + SMALL_ROWS + 1]
    half_rows = channels // (2 * heads)
    head = (lax.broadcasted_iota(jnp.int32, (heads, channels), 1) // half_rows) % heads
    pick = (head == lax.broadcasted_iota(jnp.int32, (heads, channels), 0)).astype(F32)
    gpw_ref[...] = lax.dot_general(
        pick,
        pw,
        (((1,), (1,)), ((), ())),
        precision=lax.Precision.HIGHEST,
        preferred_element_type=F32,
    )
    for h in range(heads):
        gtok_ref[h] = jnp.sum(tok * pick[h : h + 1])


def per_device(
    act,
    grad_out,
    pair,
    w_query,
    w_key,
    w_value,
    w_gate,
    w_out,
    w_pair,
    w_token,
    offsets,
    atom_token,
    padding,
):
    samples, atoms, channels = act.shape
    windows = offsets.shape[0]
    win_rows = atoms // windows
    span = pair.shape[-1]
    cp, heads = w_pair.shape
    half_rows = win_rows // 2
    lanes = heads * win_rows
    ranges = lax.axis_size("atoms")
    cores = lax.axis_size("samples")
    assert cores == 2 and ranges & (ranges - 1) == 0
    tok = atom_token.reshape(atoms // span, span)
    w_pair_t = w_pair.T
    vmem = pl.BlockSpec(memory_space=pltpu.VMEM)
    smem = pl.BlockSpec(memory_space=pltpu.SMEM)
    hbm = pl.BlockSpec(memory_space=pl.ANY)

    exchanges = [
        [pair for i in range(first, ranges - 1, 2) for pair in ((i, i + 1), (i + 1, i))]
        for first in range(2)
    ]
    last_block = atoms // span - 1
    to_send = pl.pallas_call(
        payload_kernel,
        out_shape=[jax.ShapeDtypeStruct((samples + 1, span, channels), BF16)] * 2,
        grid=(1,),
        in_specs=[
            pl.BlockSpec((samples, span, channels), lambda i: (0, last_block, 0)),
            pl.BlockSpec((samples, span, channels), lambda i: (0, 0, 0)),
            vmem,
            smem,
        ],
        out_specs=[vmem, vmem],
    )(act, act, tok, padding)
    halos = [lax.ppermute(part, "atoms", swaps) for part, swaps in zip(to_send, exchanges)]

    out_half = 5 * channels // 2
    part_rows = out_half + SMALL_ROWS
    coded_rows = part_rows + SMALL_ROWS
    geo = (samples, atoms, channels, heads, win_rows, span, cp, out_half)
    pair_flat = pair.reshape(windows, win_rows * cp, span)
    width = heads * half_rows
    common = (
        offsets,
        padding,
        w_token,
        tok,
        act,
        grad_out,
        pair_flat,
        w_query,
        w_key,
        w_value,
        w_gate,
        w_out,
        w_pair_t,
    )
    shape = jax.ShapeDtypeStruct

    def call(sides, halos=(), acc_in=None, last=False):
        edge, chained = len(halos) > 0, acc_in is not None
        args = common + tuple(halos) + ((acc_in,) if chained else ())
        in_specs = [smem] * 3 + [vmem] + [hbm] * 3 + [vmem] * 6 + [hbm] * len(halos)
        in_specs += [vmem] * chained
        count = sum(side.count for side in sides)
        queries, rows = sides[0].queries, sides[0].rows
        blocks = len(sides) * samples
        own_rows = [sum(p[2] for p in side.pieces if p[0] == "act") for side in sides]
        out_shape = [shape((samples, n, channels), BF16) for n in own_rows]
        if edge:
            out_shape += [shape((samples, span, channels), BF16)] * 2
        if last:
            out_shape += [shape((part_rows, channels), F32), shape((coded_rows, channels), BF16)]
        else:
            out_shape += [shape((2, part_rows, channels), F32)]
        out_specs = [hbm] * (len(own_rows) + 2 * edge) + [vmem] * (1 + last) + [hbm] * 2
        out_shape += [shape((count, width, span), F32), shape((count, width, span), BF16)]
        per_query = (blocks, queries, channels)
        scratch = [
            pltpu.VMEM((count, win_rows * cp, span), BF16),
            pltpu.SemaphoreType.DMA((len(sides) + 2,)),
            pltpu.VMEM((win_rows * cp, lanes), BF16),
            pltpu.VMEM((win_rows * cp, lanes), F32),
            pltpu.VMEM((atoms + 2 * span, span), F32),
            pltpu.VMEM((span // win_rows, -(-atoms // span // 8) * 8, lanes), F32),
            pltpu.VMEM((2, CODE_ROWS, span), BF16),
            pltpu.VMEM((blocks, rows, channels), BF16),
            pltpu.VMEM(per_query, BF16),
            pltpu.SemaphoreType.DMA((len(sides), 4, 3)),
            pltpu.VMEM(per_query, BF16),
            pltpu.VMEM(per_query, BF16),
            pltpu.VMEM(per_query, F32),
            pltpu.VMEM(per_query, F32),
            pltpu.VMEM(per_query, BF16),
            pltpu.VMEM(per_query, BF16),
            pltpu.VMEM(per_query, BF16),
            pltpu.VMEM((2, span, lanes), F32),
            pltpu.VMEM((2, span, lanes), F32),
        ]
        if last:
            scratch += [pltpu.VMEM((2, part_rows, channels), F32)]
        if edge:
            scratch += [
                pltpu.VMEM((2, samples, span, channels), BF16),
            ]
        scratch += [pltpu.VMEM((samples, n, channels), BF16) for n in own_rows]
        scratch += [
            pltpu.VMEM((count, width, span), F32),
            pltpu.VMEM((count, width, span), BF16),
            pltpu.SemaphoreType.DMA((len(sides) + 2 + 2 * edge,)),
        ]
        scratch += [pltpu.VMEM((rows, channels), F32)] * (4 * blocks)
        units = 6 * count * samples + 8 * count + 14 * blocks
        return pl.pallas_call(
            functools.partial(attention_kernel, geo, sides, edge, chained, last),
            out_shape=out_shape,
            in_specs=in_specs,
            out_specs=out_specs,
            scratch_shapes=scratch,
            compiler_params=pltpu.CompilerParams(vmem_limit_bytes=VMEM_LIMIT),
            cost_estimate=pl.CostEstimate(
                flops=2 * units * 128 * 128 * 128 * 4,
                bytes_accessed=12_000_000,
                transcendentals=count * samples * span * lanes,
            ),
        )(*args)

    edge_count = span // win_rows
    early_count = (windows - 2 * edge_count) * EARLY_SHARE // 12
    early = tuple(range(edge_count, edge_count + early_count))
    late = tuple(range(edge_count + early_count, windows - edge_count))
    low, high = tuple(range(edge_count)), tuple(range(windows - edge_count, windows))
    early_end = (early[-1] + 1) * win_rows + span
    late_first = late[0] * win_rows - span
    own = edge_count * win_rows + span
    swap = [(0, 1), (1, 0)]

    early_side = Side(early, win_rows, early_end, [("act", 0, early_end, 0)], 0)
    ga_early, acc, mine1, other1 = call([early_side])
    recv1 = lax.ppermute(other1, "samples", swap)

    low_side = Side(low, win_rows, own + span, [("lo", 0, span, 0), ("act", 0, own, span)], -span)
    high_side = Side(
        high,
        win_rows,
        own + span,
        [("act", atoms - own, own, 0), ("hi", 0, span, own)],
        atoms - own,
    )
    ga_low, ga_high, ga_a, ga_b, acc, mine2, other2 = call([low_side, high_side], halos, acc)
    recv2 = lax.ppermute(other2, "samples", swap)
    from_a, from_b = [
        lax.ppermute(part, "atoms", swaps) for part, swaps in zip((ga_a, ga_b), exchanges)
    ]

    late_rows = atoms - late_first
    late_side = Side(
        late, win_rows, late_rows, [("act", late_first, late_rows, 0)], late_first
    )
    ga_late, acc_mine, acc_other, mine3, other3 = call([late_side], (), acc, True)

    wide = out_half

    def encode(value):
        top = lax.reduce_precision(value, 8, 7)
        return jnp.concatenate([top, value[wide:] - top[wide:]]).astype(BF16)

    def decode(sent):
        sent = sent.astype(F32)
        return jnp.concatenate(
            [sent[:wide], sent[wide : wide + SMALL_ROWS] + sent[wide + SMALL_ROWS :]]
        )

    acc_other, other3, from_a, from_b = lax.optimization_barrier(
        (acc_other, other3, from_a, from_b)
    )
    recv3 = lax.ppermute(other3, "samples", swap)
    total = acc_mine + decode(lax.ppermute(acc_other, "samples", swap))
    def sum_pair(mine3):
        return pl.pallas_call(
            functools.partial(pair_kernel, order=(early, low + high, late), heads=heads, cp=cp),
            out_shape=shape((windows, half_rows * cp, span), BF16),
            in_specs=[vmem] * 7,
            out_specs=vmem,
            compiler_params=pltpu.CompilerParams(vmem_limit_bytes=VMEM_LIMIT),
            cost_estimate=pl.CostEstimate(
                flops=2 * windows * 256 * 256 * 256, bytes_accessed=4_000_000, transcendentals=0
            ),
        )(w_pair_t, mine1, recv1, mine2, recv2, mine3, recv3)

    def sum_act(ga_late):
        pieces = [
            (0, ga_early),
            (late_first, ga_late),
            (0, ga_low),
            (atoms - own, ga_high),
        ]
        parts = [part for _, part in pieces] + [from_a, from_b]
        return pl.pallas_call(
            functools.partial(act_sum_kernel, [first for first, _ in pieces]),
            out_shape=shape((samples, atoms, channels), BF16),
            grid=(2,),
            in_specs=[
                pl.BlockSpec((samples // 2,) + part.shape[1:], lambda s: (s, 0, 0))
                for part in parts
            ],
            out_specs=pl.BlockSpec((samples // 2, atoms, channels), lambda s: (s, 0, 0)),
            compiler_params=pltpu.CompilerParams(vmem_limit_bytes=VMEM_LIMIT),
            cost_estimate=pl.CostEstimate(
                flops=4 * samples * atoms * channels, bytes_accessed=6_000_000, transcendentals=0
            ),
        )(*parts)

    step = ranges // 2
    grad_pair = grad_act = None
    while step >= 1:
        sent = encode(total)
        if grad_pair is None:
            sent, mine3 = lax.optimization_barrier((sent, mine3))
            grad_pair = sum_pair(mine3)
        elif grad_act is None:
            sent, ga_late = lax.optimization_barrier((sent, ga_late))
            grad_act = sum_act(ga_late)
        got = lax.ppermute(sent, "atoms", [(i, i ^ step) for i in range(ranges)])
        total = decode(sent) + decode(got)
        if step == ranges // 2:
            total, grad_pair = lax.optimization_barrier((total, grad_pair))
        elif step == ranges // 4:
            total, grad_act = lax.optimization_barrier((total, grad_act))
        step //= 2
    if grad_pair is None:
        grad_pair = sum_pair(mine3)
    if grad_act is None:
        grad_act = sum_act(ga_late)
    sent = encode(total)
    got = lax.ppermute(sent, "samples", swap)
    grad_weights, grad_pair_weight, grad_token_weight = pl.pallas_call(
        functools.partial(finish_kernel, heads=heads),
        out_shape=[
            shape((5 * channels, channels), F32),
            shape((heads, cp), F32),
            shape((heads,), F32),
        ],
        in_specs=[vmem, vmem],
        out_specs=[vmem, vmem, smem],
    )(sent, got)

    return (
        grad_act,
        grad_pair.reshape(windows, half_rows, cp, span),
        grad_weights.reshape(5, channels, channels),
        grad_pair_weight.T,
        grad_token_weight,
    )


def solution(mesh):
    in_specs = (
        P("samples", ("groups", "atoms"), None),
        P("samples", ("groups", "atoms"), None),
        P(("groups", "atoms"), None, None, None),
        P(),
        P(),
        P(),
        P(),
        P(),
        P(),
        P(),
        P(("groups", "atoms")),
        P(("groups", "atoms")),
        P(("groups", "atoms")),
    )
    out_specs = (
        P("samples", ("groups", "atoms"), None),
        P(("groups", "atoms"), "samples", None, None),
        P("groups", None, None),
        P("groups", None),
        P("groups"),
    )
    return jax.shard_map(
        per_device, mesh=mesh, in_specs=in_specs, out_specs=out_specs, check_vma=False
    )
```
